32 devices in a mesh: bx: 2 (over x), by: 4 (over z), bz: 4 (over y, core).
Axes of the slice: x: 2, y: 2, z: 4, core: 2. Of those that a mesh axis runs over, the one named last changes fastest.
Arguments:
- estimate: float32 [32, 64, 512], P('bx', 'by', 'bz'), may hold values from 0.5 to 2
- raw_views: float32 [6, 32, 64, 512], P(None, 'bx', 'by', 'bz'), may hold values from 0.25 to 4
- psf: float32 [6, 3, 31], replicated, may hold values from 0.05 to 1
- offsets: int32 [6, 3], replicated, may hold values from -8 to 8, as said below
- coverage: int32 [6, 2, 4, 4], P(None, 'bx', 'by', 'bz'), may hold values from 0 to 1, as said below
Outputs:
- restored: float32 [32, 64, 512], P('bx', 'by', 'bz')
The draws below stay inside these ranges and needn't reach their ends.
Inputs may be any that keep to these rules, and one draw needn't show every extreme that they name: `offsets`: one view has first component exactly 8 and the next view (cyclically) third component exactly -8. `coverage`: every output block is covered by at least one view.
All inputs are finite; a program needn't handle non-finite values.
Results may differ from the reference program's by a relative error of at most 0.0001.
Values sent between devices are 32-bit elements; how exact they have to be, the bound alone decides.
A program may use at most 128 MiB of HBM per device.

```python
import math
import jax
import jax.numpy as jnp
from jax import lax

V = 6
K = 31
R = 15
OFF = 8
ITERS = 1
CX = 16
CY = 16
CZ = 128
NX = 32
NY = 64
NZ = 512
N_BX = 2
N_BY = 4
N_BZ = 4


def draw_offsets(key, part):
    key = jax.random.fold_in(key, 11)
    first, second = jax.random.split(key, 2)
    values = jax.random.randint(first, (V, 3), -OFF, OFF + 1)
    chosen = jax.random.randint(second, (), 0, V)
    values = values.at[chosen, 0].set(OFF)
    values = values.at[(chosen + 1) % V, 2].set(-OFF)
    return values.astype(jnp.int32)


def draw_coverage(key, part):
    key = jax.random.fold_in(key, 23)
    first, second = jax.random.split(key, 2)
    base = jax.random.randint(first, (V, N_BX, N_BY, N_BZ), 0, 2)
    chosen = jax.random.randint(second, (N_BX, N_BY, N_BZ), 0, V)
    forced = (jnp.arange(V, dtype=jnp.int32)[:, None, None, None] == chosen[None]).astype(jnp.int32)
    return jnp.maximum(base, forced).astype(jnp.int32)


def levels(key, dims, cuts, low, largest):
    loudness = 1.0
    for dim, blocks in cuts:
        steps = jax.random.uniform(jax.random.fold_in(jax.random.fold_in(key, 6), dim), (blocks,), jnp.float32, low / len(cuts), largest / len(cuts))
        loudness = loudness * jnp.repeat(jnp.exp(steps), dims[dim] // blocks).reshape((-1,) + (1,) * (len(dims) - 1 - dim))
    return loudness


def setup_inputs(seed: int = 0) -> dict:
    keys = jax.random.split(jax.random.key(seed), 6)
    estimate = jnp.clip(jnp.exp(math.log(2.0) - 1.3862944 * jax.random.uniform(keys[0], (NX, NY, NZ), jnp.float32) ** levels(keys[0], (NX, NY, NZ), ((0, 2), (1, 4), (2, 4)), -0.2, 0.2)), 0.5, 2.0)
    raw_views = jnp.clip(jnp.exp(math.log(4.0) - 2.7725887 * jax.random.uniform(keys[1], (V, NX, NY, NZ), jnp.float32) ** levels(keys[1], (V, NX, NY, NZ), ((1, 2), (2, 4), (3, 4)), -0.2, 0.2)), 0.25, 4.0)
    psf = jnp.clip(jnp.exp(jax.random.uniform(keys[2], (V, 3, K), jnp.float32, math.log(0.05), math.log(1.0))), 0.05, 1.0)
    offsets = draw_offsets(jax.random.fold_in(keys[5], 71), 0)
    coverage = draw_coverage(jax.random.fold_in(keys[5], 71), 0)
    return dict(estimate=estimate, raw_views=raw_views, psf=psf, offsets=offsets, coverage=coverage)


def along_axis(field, kernel, axis):
    moved = jnp.moveaxis(field, axis, -1)
    shape = moved.shape
    flat = moved.reshape(-1, 1, shape[-1])
    result = lax.conv_general_dilated(flat, kernel.reshape(1, 1, -1), (1,), [(R, R)], precision=lax.Precision.HIGHEST)
    return jnp.moveaxis(result.reshape(shape), -1, axis)


def blur(field, kernels, flipped):
    for axis in range(3):
        kernel = kernels[axis]
        if flipped:
            kernel = jnp.flip(kernel)
        field = along_axis(field, kernel, axis)
    return field


def reference(estimate, raw_views, psf, offsets, coverage):
    kernels = psf / jnp.sum(psf, axis=2, keepdims=True)
    observed = []
    masks = []
    weights = jnp.zeros((NX, NY, NZ), jnp.float32)
    for view in range(V):
        padded = jnp.pad(raw_views[view], OFF)
        starts = (OFF + offsets[view, 0], OFF + offsets[view, 1], OFF + offsets[view, 2])
        observed.append(lax.dynamic_slice(padded, starts, (NX, NY, NZ)))
        blocks = coverage[view].astype(jnp.float32)[:, None, :, None, :, None]
        mask = jnp.broadcast_to(blocks, (N_BX, CX, N_BY, CY, N_BZ, CZ)).reshape(NX, NY, NZ)
        masks.append(mask)
        weights = weights + blur(mask, kernels[view], True)
    restored = estimate
    for step in range(ITERS):
        total = jnp.zeros((NX, NY, NZ), jnp.float32)
        for view in range(V):
            ratio = masks[view] * observed[view] / blur(restored, kernels[view], False)
            total = total + blur(ratio, kernels[view], True)
        restored = restored * total / weights
    return restored
```

```python
import functools

import jax
import jax.numpy as jnp
from jax import lax
from jax.experimental import pallas as pl
from jax.experimental.pallas import tpu as pltpu
from jax.sharding import PartitionSpec as P

F32 = jnp.float32
BF16 = jnp.bfloat16
MESH = pl.DeviceIdType.MESH
OFF = 8
TAPS = 31
REACH = 15
VIEWS = 6
SX = 16
SY = 16
SZ = 128
XY = SX * SY
LOW, LOW_COV, OWN, OWN_COV, HIGH, HIGH_COV, ROWS = 0, 16, 24, 152, 160, 176, 256


def split(value):
    high = value.astype(BF16)
    return high, (value - high.astype(F32)).astype(BF16)


def dot(a, b):
    return jnp.dot(a, b, preferred_element_type=F32)


def dot3(a_high, a_low, b_high, b_low):
    return dot(a_high, b_high) + (dot(a_high, b_low) + dot(a_low, b_high))


def iota(shape, dim):
    return lax.broadcasted_iota(jnp.int32, shape, dim)


def kernel(
    counts, est, raw, psf_s, psf_v, offsets, coverage, out,
    wide, wide_h, wide_l, rx, ry, rz, kn,
    kron_h, kron_l, kront_h, kront_l, fz_h, fz_l, bz_h, bz_l,
    blurred, back_h, back_l, spread, from_z, from_y, from_x, weights, send, recv,
):
    nx, ny, nz = counts
    xslots = 2 if nx == 2 else 3
    group = xslots * XY
    lanes = 3 * group
    ix, iy, iz = lax.axis_index("bx"), lax.axis_index("by"), lax.axis_index("bz")
    where = {"bx": (ix, nx), "by": (iy, ny), "bz": (iz, nz)}
    has_left = {name: i > 0 for name, (i, n) in where.items()}
    has_right = {name: i < n - 1 for name, (i, n) in where.items()}
    x_shift = [0, 1 - 2 * ix] if nx == 2 else [0, -1, 1]
    y_shift = [0, -1, 1]
    x_left_slot = 1
    x_right_slot = 1 if nx == 2 else 2

    def to_left(axis, index, src, dst):
        return axis, True, pltpu.make_async_remote_copy(
            src_ref=src, dst_ref=dst, send_sem=send.at[index], recv_sem=recv.at[index],
            device_id={axis: where[axis][0] - 1}, device_id_type=MESH,
        )

    def to_right(axis, index, src, dst):
        return axis, False, pltpu.make_async_remote_copy(
            src_ref=src, dst_ref=dst, send_sem=send.at[index], recv_sem=recv.at[index],
            device_id={axis: where[axis][0] + 1}, device_id_type=MESH,
        )

    def start(copies):
        for axis, left, copy in copies:
            @pl.when(has_left[axis] if left else has_right[axis])
            def _():
                copy.start()

    def arrive(copies):
        for axis, left, copy in copies:
            @pl.when(has_right[axis] if left else has_left[axis])
            def _():
                copy.wait_recv()

    def sent(copies):
        for axis, left, copy in copies:
            @pl.when(has_left[axis] if left else has_right[axis])
            def _():
                copy.wait_send()

    def absent(axis, left, ref, index):
        @pl.when(jnp.logical_not(has_left[axis] if left else has_right[axis]))
        def _():
            ref[index] = jnp.zeros(ref.at[index].shape, ref.dtype)

    full = slice(None)
    own_rows = slice(OWN, OWN_COV + 8)

    wide[OWN:OWN_COV, 0:XY] = est[...].reshape(XY, SZ).T
    cov_rows = jnp.zeros((8, XY), F32)
    for view in range(VIEWS):
        value = coverage[view, 0, 0, 0].astype(F32)
        cov_rows = jnp.where(iota((8, XY), 0) == view, value, cov_rows)
    wide[OWN_COV : OWN_COV + 8, 0:XY] = cov_rows
    wide[HIGH_COV + 8 : ROWS, :] = jnp.zeros((ROWS - HIGH_COV - 8, lanes), F32)
    if nx > 2:
        absent("bx", True, wide, (own_rows, slice(XY, 2 * XY)))
        absent("bx", False, wide, (own_rows, slice(2 * XY, 3 * XY)))
    absent("by", True, wide, (own_rows, slice(group, 2 * group)))
    absent("by", False, wide, (own_rows, slice(2 * group, 3 * group)))
    absent("bz", True, wide, (slice(LOW, OWN), full))
    absent("bz", False, wide, (slice(HIGH, HIGH_COV + 8), full))
    absent("bx", True, rx, (full, slice(0, 8), full, full))
    absent("bx", False, rx, (full, slice(24, 32), full, full))
    absent("by", True, ry, (full, full, slice(0, 8), full))
    absent("by", False, ry, (full, full, slice(24, 32), full))
    absent("bz", True, rz, (full, slice(0, 8), full))
    absent("bz", False, rz, (full, slice(136, 144), full))
    rx[:, 8:24] = raw[...]

    barrier = pltpu.get_barrier_semaphore()
    for axis, (i, n) in where.items():
        @pl.when(has_left[axis])
        def _():
            pl.semaphore_signal(barrier, inc=1, device_id={axis: i - 1}, device_id_type=MESH)

        @pl.when(has_right[axis])
        def _():
            pl.semaphore_signal(barrier, inc=1, device_id={axis: i + 1}, device_id_type=MESH)
    degree = sum(
        (has_left[axis].astype(jnp.int32) + has_right[axis].astype(jnp.int32) for axis in where),
        jnp.int32(0),
    )
    pl.semaphore_wait(barrier, degree)

    def lane_slot(slot):
        return slice(slot * XY, (slot + 1) * XY)

    est_x = [
        to_left("bx", 0, wide.at[own_rows, 0:XY], wide.at[own_rows, lane_slot(x_right_slot)]),
        to_right("bx", 1, wide.at[own_rows, 0:XY], wide.at[own_rows, lane_slot(x_left_slot)]),
    ]
    est_y = [
        to_left("by", 2, wide.at[own_rows, 0:group], wide.at[own_rows, 2 * group : 3 * group]),
        to_right("by", 3, wide.at[own_rows, 0:group], wide.at[own_rows, group : 2 * group]),
    ]
    est_z = [
        to_left("bz", 4, wide.at[OWN : OWN + 16], wide.at[HIGH : HIGH + 16]),
        to_left("bz", 5, wide.at[OWN_COV : OWN_COV + 8], wide.at[HIGH_COV : HIGH_COV + 8]),
        to_right("bz", 6, wide.at[OWN_COV - 16 : OWN_COV + 8], wide.at[LOW : LOW + 24]),
    ]
    raw_x = [
        to_left("bx", 7, rx.at[:, 8:16], rx.at[:, 24:32]),
        to_right("bx", 8, rx.at[:, 16:24], rx.at[:, 0:8]),
    ]
    raw_y = [
        to_left("by", 9, ry.at[:, :, 8:16], ry.at[:, :, 24:32]),
        to_right("by", 10, ry.at[:, :, 16:24], ry.at[:, :, 0:8]),
    ]
    raw_z = [
        to_left("bz", 11, rz.at[:, 8:16], rz.at[:, 136:144]),
        to_right("bz", 12, rz.at[:, 128:136], rz.at[:, 0:8]),
    ]

    def toeplitz(view, axis, places, total):
        result = [jnp.zeros(place.shape, F32) for place in places]
        for tap in range(TAPS):
            value = psf_s[view, axis, tap]
            result = [jnp.where(p == tap, value, r) for p, r in zip(places, result)]
        return [r / jnp.full(r.shape, total, F32) for r in result]

    def build(first, last):
        @pl.loop(first, last)
        def _(view):
            totals = []
            for axis in range(3):
                total = psf_s[view, axis, 0]
                for tap in range(1, TAPS):
                    total = total + psf_s[view, axis, tap]
                totals.append(total)
            row, lane = iota((16, XY), 0), iota((16, XY), 1)
            lane_x, lane_y = lane // SY, lane % SY
            x_to = [REACH + SX * d + lane_x - row for d in x_shift]
            x_from = [REACH + SX * d + row - lane_x for d in x_shift]
            y_to = [REACH + SY * d + lane_y - row for d in y_shift]
            y_from = [REACH + SY * d + row - lane_y for d in y_shift]
            xs = toeplitz(view, 0, x_to + x_from, totals[0])
            ys = toeplitz(view, 1, y_to + y_from, totals[1])
            for y in range(3):
                for x in range(xslots):
                    base = y * group + x * XY
                    for i in range(16):
                        high, low = split(ys[y] * xs[x][i : i + 1, :])
                        kron_h[view, i * 16 : (i + 1) * 16, base : base + XY] = high
                        kron_l[view, i * 16 : (i + 1) * 16, base : base + XY] = low
                        high, low = split(ys[3 + y] * xs[xslots + x][i : i + 1, :])
                        kront_h[view, base + i * 16 : base + (i + 1) * 16, :] = high
                        kront_l[view, base + i * 16 : base + (i + 1) * 16, :] = low
            row, lane = iota((SZ, ROWS), 0), iota((SZ, ROWS), 1)
            place = jnp.where(
                lane < LOW_COV, lane - 16,
                jnp.where(
                    (lane >= OWN) & (lane < OWN_COV), lane - OWN,
                    jnp.where((lane >= HIGH) & (lane < HIGH_COV), lane - HIGH + SZ, 10000),
                ),
            )
            (matrix,) = toeplitz(view, 2, [REACH + place - row], totals[2])
            fz_h[view], fz_l[view] = split(matrix)
            row, lane = iota((SZ + 32, SZ), 0), iota((SZ + 32, SZ), 1)
            (matrix,) = toeplitz(view, 2, [REACH - 16 + row - lane], totals[2])
            bz_h[view], bz_l[view] = split(matrix)

    start(est_x)
    start(raw_x)
    kn[...] = jnp.zeros(kn.shape, F32)
    for axis in range(3):
        values = psf_v[:, axis, :]
        kn[axis, 0:VIEWS, 0:TAPS] = values / jnp.sum(values, axis=1, keepdims=True)
    arrive(est_x)
    start(est_y)
    build(0, 3)
    arrive(raw_x)

    @pl.loop(0, VIEWS)
    def _(view):
        ry[view, :, 8:24, :] = rx[view, pl.ds(OFF + offsets[view, 0], SX), :, :]

    start(raw_y)
    arrive(est_y)
    start(est_z)
    build(3, VIEWS)
    arrive(est_z)

    highest = lax.Precision.HIGHEST
    tap, lane = iota((128, XY), 0), iota((128, XY), 1)
    lane_x, lane_y = lane // SY, lane % SY

    def factor(axis, position, shift, size):
        cell = position + REACH - tap[:, : position.shape[1]] - shift * size
        inside = ((cell >= 0) & (cell < size)).astype(F32)
        return jnp.dot(kn[axis], inside, precision=highest, preferred_element_type=F32)

    factor_x = [factor(0, lane_x, d, SX) for d in x_shift]
    factor_y = [factor(1, lane_y, d, SY) for d in y_shift]
    factor_z = [factor(2, lane[:, :SZ], d, SZ) for d in (-1, 0, 1)]
    rows = []
    for base in (LOW_COV, OWN_COV, HIGH_COV):
        total = jnp.zeros((8, XY), F32)
        for y in range(3):
            part = jnp.zeros((8, XY), F32)
            for x in range(xslots):
                first = y * group + x * XY
                part = part + wide[base : base + 8, first : first + XY] * factor_x[x]
            total = total + part * factor_y[y]
        rows.append(total)
    weights[...] = jnp.dot(
        jnp.concatenate(factor_z, axis=0).T, jnp.concatenate(rows, axis=0),
        precision=highest, preferred_element_type=F32,
    )

    wide_h[...], wide_l[...] = split(wide[...])

    @pl.loop(0, VIEWS)
    def _(view):
        total = jnp.zeros((SZ, XY), F32)
        for y in range(3):
            cut = slice(y * group, (y + 1) * group)
            high, low = split(dot3(fz_h[view], fz_l[view], wide_h[:, cut], wide_l[:, cut]))
            total = total + dot3(high, low, kront_h[view, cut, :], kront_l[view, cut, :])
        blurred[view] = total

    arrive(raw_y)

    @pl.loop(0, VIEWS)
    def _(view):
        turn = lax.rem(32 - OFF - offsets[view, 1], 32)
        shifted = pltpu.roll(ry[view], turn, 1)[:, 0:SY, :]
        rz[view, 8:136, :] = shifted.reshape(XY, SZ).T

    start(raw_z)
    arrive(raw_z)

    @pl.loop(0, VIEWS)
    def _(view):
        turn = lax.rem(SZ + 16 - OFF - offsets[view, 2], SZ + 16)
        observed = pltpu.roll(rz[view], turn, 0)[0:SZ, :]
        mask = coverage[view, 0, 0, 0].astype(F32)
        high, low = split(mask * observed / blurred[view])
        rows_of = pl.ds(pl.multiple_of(view * SZ, SZ), SZ)
        for y in range(3):
            cut = slice(y * group, (y + 1) * group)
            part = dot3(high, low, kron_h[view, :, cut], kron_l[view, :, cut])
            back_h[rows_of, cut], back_l[rows_of, cut] = split(part)

    for y in range(3):
        cut = slice(y * group, (y + 1) * group)
        total = jnp.zeros((SZ + 32, group), F32)
        for view in range(VIEWS):
            rows_of = slice(view * SZ, (view + 1) * SZ)
            total = total + dot3(bz_h[view], bz_l[view], back_h[rows_of, cut], back_l[rows_of, cut])
        spread[:, cut] = total

    back_z = [
        to_left("bz", 13, spread.at[0:16], from_z.at[1]),
        to_right("bz", 14, spread.at[SZ + 16 : SZ + 32], from_z.at[0]),
    ]
    absent("bz", True, from_z, (0, full, full))
    absent("bz", False, from_z, (1, full, full))
    absent("by", True, from_y, (0, full, full))
    absent("by", False, from_y, (1, full, full))
    absent("bx", True, from_x, (0, full, full))
    absent("bx", False, from_x, (1, full, full))
    start(back_z)
    arrive(back_z)
    spread[16:32, :] = spread[16:32, :] + from_z[0]
    spread[SZ : SZ + 16, :] = spread[SZ : SZ + 16, :] + from_z[1]
    mid = slice(16, SZ + 16)
    back_y = [
        to_left("by", 15, spread.at[mid, group : 2 * group], from_y.at[1]),
        to_right("by", 16, spread.at[mid, 2 * group : 3 * group], from_y.at[0]),
    ]
    start(back_y)
    arrive(back_y)
    spread[mid, 0:group] = spread[mid, 0:group] + from_y[0] + from_y[1]
    back_x = [
        to_left("bx", 17, spread.at[mid, lane_slot(x_left_slot)], from_x.at[1]),
        to_right("bx", 18, spread.at[mid, lane_slot(x_right_slot)], from_x.at[0]),
    ]
    start(back_x)
    arrive(back_x)
    total = spread[mid, 0:XY] + from_x[0] + from_x[1]
    restored = wide[OWN:OWN_COV, 0:XY] * total / weights[...]
    out[...] = restored.T.reshape(SX, SY, SZ)
    for copies in (est_x, est_y, est_z, raw_x, raw_y, raw_z, back_z, back_y, back_x):
        sent(copies)


def on_device(counts, estimate, raw_views, psf, offsets, coverage):
    xslots = 2 if counts[0] == 2 else 3
    group = xslots * XY
    lanes = 3 * group
    vmem = pl.BlockSpec(memory_space=pltpu.VMEM)
    smem = pl.BlockSpec(memory_space=pltpu.SMEM)
    return pl.pallas_call(
        functools.partial(kernel, counts),
        out_shape=jax.ShapeDtypeStruct(estimate.shape, F32),
        in_specs=[vmem, vmem, smem, vmem, smem, smem],
        out_specs=vmem,
        scratch_shapes=[
            pltpu.VMEM((ROWS, lanes), F32),
            pltpu.VMEM((ROWS, lanes), BF16),
            pltpu.VMEM((ROWS, lanes), BF16),
            pltpu.VMEM((VIEWS, 32, SY, SZ), F32),
            pltpu.VMEM((VIEWS, SX, 32, SZ), F32),
            pltpu.VMEM((VIEWS, SZ + 16, XY), F32),
            pltpu.VMEM((3, 8, 128), F32),
            pltpu.VMEM((VIEWS, XY, lanes), BF16),
            pltpu.VMEM((VIEWS, XY, lanes), BF16),
            pltpu.VMEM((VIEWS, lanes, XY), BF16),
            pltpu.VMEM((VIEWS, lanes, XY), BF16),
            pltpu.VMEM((VIEWS, SZ, ROWS), BF16),
            pltpu.VMEM((VIEWS, SZ, ROWS), BF16),
            pltpu.VMEM((VIEWS, SZ + 32, SZ), BF16),
            pltpu.VMEM((VIEWS, SZ + 32, SZ), BF16),
            pltpu.VMEM((VIEWS, SZ, XY), F32),
            pltpu.VMEM((VIEWS * SZ, lanes), BF16),
            pltpu.VMEM((VIEWS * SZ, lanes), BF16),
            pltpu.VMEM((SZ + 32, lanes), F32),
            pltpu.VMEM((2, 16, lanes), F32),
            pltpu.VMEM((2, SZ, group), F32),
            pltpu.VMEM((2, SZ, XY), F32),
            pltpu.VMEM((SZ, XY), F32),
            pltpu.SemaphoreType.DMA((19,)),
            pltpu.SemaphoreType.DMA((19,)),
        ],
        compiler_params=pltpu.CompilerParams(
            collective_id=0, has_side_effects=True, vmem_limit_bytes=56 * 1024 * 1024
        ),
    )(estimate, raw_views, psf, psf, offsets, coverage)


def solution(mesh):
    counts = (mesh.shape["bx"], mesh.shape["by"], mesh.shape["bz"])
    return jax.shard_map(
        functools.partial(on_device, counts),
        mesh=mesh,
        in_specs=(
            P("bx", "by", "bz"),
            P(None, "bx", "by", "bz"),
            P(),
            P(),
            P(None, "bx", "by", "bz"),
        ),
        out_specs=P("bx", "by", "bz"),
        check_vma=False,
    )
```

```python
import functools

import jax
import jax.numpy as jnp
from jax import lax
from jax.experimental import pallas as pl
from jax.experimental.pallas import tpu as pltpu
from jax.sharding import PartitionSpec as P

F32 = jnp.float32
BF16 = jnp.bfloat16
MESH = pl.DeviceIdType.MESH
OFF = 8
TAPS = 31
REACH = 15
VIEWS = 6
SEMAPHORES = 48
SX = 16
SY = 16
SZ = 128
XY = SX * SY
HIGH, GAP, LOW, ROWS = SZ, SZ + 16, 240, 256
WIDE = SZ + 32


def split(value):
    high = value.astype(BF16)
    return high, (value - high.astype(F32)).astype(BF16)


def dot(a, b):
    return jnp.dot(a, b, preferred_element_type=F32)


def iota(shape, dim):
    return lax.broadcasted_iota(jnp.int32, shape, dim)


def dot3(stack, b_high, b_low):
    half = stack.shape[0] // 2
    both = dot(stack, b_high)
    return both[:half] + (both[half:] + dot(stack[:half], b_low))


def kernel(
    counts, est, raw, psf_s, psf_v, offsets, coverage, out,
    wide, wide_h, wide_l, cov, rx_a, rx_b, ry_a, ry_b, rz, kn, knz, scale,
    kron_h, kron_l, kront_h, kront_l, fz, bz,
    blurred, ratio, back_h, back_l, spread, from_x, from_y, from_z, weights, send, recv,
):
    nx, ny, nz = counts
    xslots = 2 if nx == 2 else 3
    group = 3 * XY
    lanes = xslots * group
    ix, iy, iz = lax.axis_index("bx"), lax.axis_index("by"), lax.axis_index("bz")
    where = {"bx": (ix, nx), "by": (iy, ny), "bz": (iz, nz)}
    has_left = {name: i > 0 for name, (i, n) in where.items()}
    has_right = {name: i < n - 1 for name, (i, n) in where.items()}
    x_shift = [0, 1 - 2 * ix] if nx == 2 else [0, -1, 1]
    y_shift = [0, -1, 1]
    x_left_slot = 1
    x_right_slot = 1 if nx == 2 else 2
    used = iter(range(SEMAPHORES))

    def to_side(axis, left, src, dst):
        index = next(used)
        return axis, left, pltpu.make_async_remote_copy(
            src_ref=src, dst_ref=dst, send_sem=send.at[index], recv_sem=recv.at[index],
            device_id={axis: where[axis][0] + (-1 if left else 1)}, device_id_type=MESH,
        )

    def to_left(axis, src, dst):
        return to_side(axis, True, src, dst)

    def to_right(axis, src, dst):
        return to_side(axis, False, src, dst)

    def start(copies):
        for axis, left, copy in copies:
            @pl.when(has_left[axis] if left else has_right[axis])
            def _():
                copy.start()

    def arrive(copies):
        for axis, left, copy in copies:
            @pl.when(has_right[axis] if left else has_left[axis])
            def _():
                copy.wait_recv()

    def sent(copies):
        for axis, left, copy in copies:
            @pl.when(has_left[axis] if left else has_right[axis])
            def _():
                copy.wait_send()

    def absent(axis, left, ref, index):
        @pl.when(jnp.logical_not(has_left[axis] if left else has_right[axis]))
        def _():
            ref[index] = jnp.zeros(ref.at[index].shape, ref.dtype)

    def block(x, y):
        return slice((3 * x + y) * XY, (3 * x + y + 1) * XY)

    full = slice(None)
    own = slice(0, SZ)

    barrier = pltpu.get_barrier_semaphore()
    for axis, (i, n) in where.items():
        @pl.when(has_left[axis])
        def _():
            pl.semaphore_signal(barrier, inc=1, device_id={axis: i - 1}, device_id_type=MESH)

        @pl.when(has_right[axis])
        def _():
            pl.semaphore_signal(barrier, inc=1, device_id={axis: i + 1}, device_id_type=MESH)

    wide[own, block(0, 0)] = est[...].reshape(XY, SZ).T
    cov_rows = jnp.zeros((8, SZ), F32)
    for view in range(VIEWS):
        value = coverage[0, view].astype(F32)
        cov_rows = jnp.where(iota((8, SZ), 0) == view, value, cov_rows)
    cov[1, 0, 0] = cov_rows

    degree = sum(
        (has_left[axis].astype(jnp.int32) + has_right[axis].astype(jnp.int32) for axis in where),
        jnp.int32(0),
    )
    pl.semaphore_wait(barrier, degree)

    half = VIEWS // 2
    first, last = slice(0, half), slice(half, VIEWS)
    est_x = [
        to_left("bx", wide.at[own, block(0, 0)], wide.at[own, block(x_right_slot, 0)]),
        to_right("bx", wide.at[own, block(0, 0)], wide.at[own, block(x_left_slot, 0)]),
        to_left("bx", cov.at[1, 0, 0], cov.at[1, 0, x_right_slot]),
        to_right("bx", cov.at[1, 0, 0], cov.at[1, 0, x_left_slot]),
    ]
    est_y = [
        [
            to_left("by", wide.at[own, block(x, 0)], wide.at[own, block(x, 2)]),
            to_right("by", wide.at[own, block(x, 0)], wide.at[own, block(x, 1)]),
        ]
        for x in range(xslots)
    ]
    cov_y = [
        to_left("by", cov.at[1, 0], cov.at[1, 2]),
        to_right("by", cov.at[1, 0], cov.at[1, 1]),
    ]
    est_z = [
        to_left("bz", wide.at[0:16], wide.at[HIGH:GAP]),
        to_right("bz", wide.at[SZ - 16 : SZ], wide.at[LOW:ROWS]),
        to_left("bz", cov.at[1], cov.at[2]),
        to_right("bz", cov.at[1], cov.at[0]),
    ]
    raw_ax = [
        to_left("bx", raw.at[first, 0:8], rx_a.at[:, 24:32]),
        to_right("bx", raw.at[first, 8:16], rx_a.at[:, 0:8]),
    ]
    raw_ay = [
        to_left("by", ry_a.at[:, :, 8:16], ry_a.at[:, :, 24:32]),
        to_right("by", ry_a.at[:, :, 16:24], ry_a.at[:, :, 0:8]),
    ]
    raw_by = [
        to_left("by", raw.at[last, :, 0:8], ry_b.at[:, :, 24:32]),
        to_right("by", raw.at[last, :, 8:16], ry_b.at[:, :, 0:8]),
    ]
    raw_bx = [
        to_left("bx", rx_b.at[:, 8:16], rx_b.at[:, 24:32]),
        to_right("bx", rx_b.at[:, 16:24], rx_b.at[:, 0:8]),
    ]
    raw_z = [
        to_left("bz", rz.at[:, 8:16], rz.at[:, 136:144]),
        to_right("bz", rz.at[:, 128:136], rz.at[:, 0:8]),
    ]

    start(est_x)
    start(est_y[0])
    start(raw_ax)
    start(raw_by)

    wide[GAP:LOW, :] = jnp.zeros((LOW - GAP, lanes), F32)
    if nx > 2:
        for left, slot in ((True, x_left_slot), (False, x_right_slot)):
            absent("bx", left, wide, (own, block(slot, 0)))
            absent("bx", left, cov, (1, 0, slot, full, full))
    for left, slot in ((True, 1), (False, 2)):
        for x in range(xslots):
            absent("by", left, wide, (own, block(x, slot)))
        absent("by", left, cov, (1, slot, full, full, full))
    absent("bz", True, wide, (slice(LOW, ROWS), full))
    absent("bz", False, wide, (slice(HIGH, GAP), full))
    absent("bz", True, cov, (0, full, full, full, full))
    absent("bz", False, cov, (2, full, full, full, full))
    for rx, ry in ((rx_a, ry_a), (rx_b, ry_b)):
        absent("bx", True, rx, (full, slice(0, 8), full, full))
        absent("bx", False, rx, (full, slice(24, 32), full, full))
        absent("by", True, ry, (full, full, slice(0, 8), full))
        absent("by", False, ry, (full, full, slice(24, 32), full))
    absent("bz", True, rz, (full, slice(0, 8), full))
    absent("bz", False, rz, (full, slice(136, 144), full))
    absent("bz", True, from_z, (0, full, full))
    absent("bz", False, from_z, (1, full, full))
    absent("by", True, from_y, (0, full, full, full))
    absent("by", False, from_y, (1, full, full, full))
    absent("bx", True, from_x, (0, full, full))
    absent("bx", False, from_x, (1, full, full))
    rx_a[:, 8:24] = raw[first]
    ry_b[:, :, 8:24] = raw[last]

    kn[...] = jnp.zeros(kn.shape, F32)
    for axis in range(3):
        values = psf_v[:, axis, :]
        total = jnp.sum(values, axis=1, keepdims=True)
        kn[axis, 0:VIEWS, 0:TAPS] = values / total
        scale[axis, 0:VIEWS, :] = jnp.broadcast_to(1.0 / total, (VIEWS, XY))
    knz[...] = pltpu.roll(kn[2], XY - REACH, 1)

    def toeplitz(view, axis, places):
        result = [jnp.zeros(place.shape, F32) for place in places]
        for tap in range(TAPS):
            value = psf_s[view, axis, tap]
            result = [jnp.where(p == tap, value, r) for p, r in zip(places, result)]
        factor = scale[axis, pl.ds(view, 1), :]
        return [r * factor for r in result]

    def build(begin, end):
        @pl.loop(begin, end)
        def _(view):
            row, lane = iota((16, XY), 0), iota((16, XY), 1)
            lane_x, lane_y = lane // SY, lane % SY
            x_to = [REACH + SX * d + lane_x - row for d in x_shift]
            x_from = [REACH + SX * d + row - lane_x for d in x_shift]
            y_to = [REACH + SY * d + lane_y - row for d in y_shift]
            y_from = [REACH + SY * d + row - lane_y for d in y_shift]
            xs = toeplitz(view, 0, x_to + x_from)
            ys = toeplitz(view, 1, y_to + y_from)
            for x in range(xslots):
                for y in range(3):
                    base = (3 * x + y) * XY
                    for i in range(16):
                        high, low = split(ys[y] * xs[x][i : i + 1, :])
                        kron_h[view, i * 16 : (i + 1) * 16, base : base + XY] = high
                        kron_l[view, i * 16 : (i + 1) * 16, base : base + XY] = low
                        high, low = split(ys[3 + y] * xs[xslots + x][i : i + 1, :])
                        kront_h[view, base + i * 16 : base + (i + 1) * 16, :] = high
                        kront_l[view, base + i * 16 : base + (i + 1) * 16, :] = low
            line = jnp.broadcast_to(knz[pl.ds(view, 1), :], (SZ, ROWS))
            band = pltpu.roll(line, 0, 1, stride=1, stride_axis=0)
            fz[view, 0:SZ], fz[view, SZ : 2 * SZ] = split(band)
            columns = pl.ds(pl.multiple_of(view * SZ, SZ), SZ)
            turned = band.T
            turned = jnp.concatenate([turned[0:GAP], turned[LOW:ROWS]], axis=0)
            bz[0:WIDE, columns], bz[WIDE : 2 * WIDE, columns] = split(turned)

    build(0, 2)
    arrive(est_x)
    for x in range(1, xslots):
        start(est_y[x])
    start(cov_y)
    build(2, 4)
    arrive(raw_ax)

    @pl.loop(0, half)
    def _(view):
        ry_a[view, :, 8:24, :] = rx_a[view, pl.ds(OFF + offsets[0, view], SX), :, :]

    start(raw_ay)

    def turned_y(ry, view, offset):
        return pltpu.roll(ry[view], lax.rem(32 - OFF - offset, 32), 1)[:, 0:SY, :]

    arrive(raw_by)

    @pl.loop(0, half)
    def _(view):
        rx_b[view, 8:24] = turned_y(ry_b, view, offsets[1, half + view])

    start(raw_bx)
    for copies in est_y:
        arrive(copies)
    arrive(cov_y)
    start(est_z)
    build(4, VIEWS)
    arrive(est_z)

    wide_h[...], wide_l[...] = split(wide[...])

    def forward(begin, end):
        @pl.loop(begin, end)
        def _(view):
            total = jnp.zeros((SZ, XY), F32)
            for x in range(xslots):
                cut = slice(x * group, (x + 1) * group)
                part = dot3(fz[view], wide_h[:, cut], wide_l[:, cut])
                stack = jnp.concatenate(split(part), axis=0)
                total = total + dot3(stack, kront_h[view, cut, :], kront_l[view, cut, :])
            blurred[view] = total

    forward(0, 4)
    arrive(raw_ay)
    arrive(raw_bx)

    @pl.loop(0, half)
    def _(view):
        rz[view, 8:136, :] = turned_y(ry_a, view, offsets[1, view]).reshape(XY, SZ).T
        shifted = rx_b[view, pl.ds(OFF + offsets[0, half + view], SX), :, :]
        rz[half + view, 8:136, :] = shifted.reshape(XY, SZ).T

    start(raw_z)
    forward(4, VIEWS)
    arrive(raw_z)

    @pl.loop(0, VIEWS)
    def _(view):
        turn = lax.rem(SZ + 16 - OFF - offsets[2, view], SZ + 16)
        observed = pltpu.roll(rz[view], turn, 0)[0:SZ, :]
        mask = coverage[0, view].astype(F32)
        ratio[view, 0:SZ], ratio[view, SZ : 2 * SZ] = split(mask * observed / blurred[view])

    back_y = [
        [
            to_left("by", spread.at[:, block(x, 1)], from_y.at[1, x]),
            to_right("by", spread.at[:, block(x, 2)], from_y.at[0, x]),
        ]
        for x in range(xslots)
    ]
    back_x = [
        to_left("bx", spread.at[:, block(x_left_slot, 0)], from_x.at[1]),
        to_right("bx", spread.at[:, block(x_right_slot, 0)], from_x.at[0]),
    ]
    back_z = [
        to_left("bz", spread.at[GAP:WIDE, block(0, 0)], from_z.at[1]),
        to_right("bz", spread.at[HIGH:GAP, block(0, 0)], from_z.at[0]),
    ]

    def add_y(x):
        arrive(back_y[x])
        spread[:, block(x, 0)] = spread[:, block(x, 0)] + (from_y[0, x] + from_y[1, x])

    for x in reversed(range(xslots)):
        cut = slice(x * group, (x + 1) * group)

        @pl.loop(0, VIEWS)
        def _(view):
            part = dot3(ratio[view], kron_h[view, :, cut], kron_l[view, :, cut])
            rows_of = pl.ds(pl.multiple_of(view * SZ, SZ), SZ)
            back_h[rows_of, :], back_l[rows_of, :] = split(part)

        for y in (1, 2, 0):
            local = slice(y * XY, (y + 1) * XY)
            spread[:, block(x, y)] = dot3(bz[...], back_h[:, local], back_l[:, local])
            if y > 0:
                start(back_y[x][y - 1 : y])
    for x in range(1, xslots):
        add_y(x)
    start(back_x)

    highest = lax.Precision.HIGHEST
    tap, lane = iota((XY, XY), 0), iota((XY, XY), 1)
    lane_x, lane_y = lane // SY, lane % SY

    def factor(axis, position, shift, size):
        cell = position + REACH - tap[:, : position.shape[1]] - shift * size
        inside = ((cell >= 0) & (cell < size)).astype(F32)
        return jnp.dot(kn[axis], inside, precision=highest, preferred_element_type=F32)

    factor_x = [factor(0, lane_x, d, SX) for d in x_shift]
    factor_y = [factor(1, lane_y, d, SY) for d in y_shift]
    factor_z = [factor(2, lane[:, :SZ], d, SZ) for d in (-1, 0, 1)]
    rows = []
    for z in range(3):
        total = jnp.zeros((8, XY), F32)
        for y in range(3):
            part = jnp.zeros((8, XY), F32)
            for x in range(xslots):
                part = part + jnp.concatenate([cov[z, y, x]] * 2, axis=1) * factor_x[x]
            total = total + part * factor_y[y]
        rows.append(total)
    weights[...] = jnp.dot(
        jnp.concatenate(factor_z, axis=0).T, jnp.concatenate(rows, axis=0),
        precision=highest, preferred_element_type=F32,
    )

    add_y(0)
    arrive(back_x)
    spread[:, block(0, 0)] = spread[:, block(0, 0)] + (from_x[0] + from_x[1])
    start(back_z)
    arrive(back_z)
    total = spread[own, block(0, 0)]
    total = jnp.concatenate(
        [total[0:16] + from_z[0], total[16 : SZ - 16], total[SZ - 16 : SZ] + from_z[1]], axis=0
    )
    restored = wide[own, block(0, 0)] * total / weights[...]
    out[...] = restored.T.reshape(SX, SY, SZ)
    for copies in [est_x, *est_y, cov_y, est_z, raw_ax, raw_ay, raw_bx, raw_by, raw_z]:
        sent(copies)
    for copies in [*back_y, back_x, back_z]:
        sent(copies)


def on_device(counts, estimate, raw_views, psf, offsets, coverage):
    xslots = 2 if counts[0] == 2 else 3
    group = 3 * XY
    lanes = xslots * group
    vmem = pl.BlockSpec(memory_space=pltpu.VMEM)
    smem = pl.BlockSpec(memory_space=pltpu.SMEM)
    return pl.pallas_call(
        functools.partial(kernel, counts),
        out_shape=jax.ShapeDtypeStruct(estimate.shape, F32),
        in_specs=[vmem, vmem, smem, vmem, smem, smem],
        out_specs=vmem,
        scratch_shapes=[
            pltpu.VMEM((ROWS, lanes), F32),
            pltpu.VMEM((ROWS, lanes), BF16),
            pltpu.VMEM((ROWS, lanes), BF16),
            pltpu.VMEM((3, 3, xslots, 8, SZ), F32),
            pltpu.VMEM((VIEWS // 2, 32, SY, SZ), F32),
            pltpu.VMEM((VIEWS // 2, 32, SY, SZ), F32),
            pltpu.VMEM((VIEWS // 2, SX, 32, SZ), F32),
            pltpu.VMEM((VIEWS // 2, SX, 32, SZ), F32),
            pltpu.VMEM((VIEWS, SZ + 16, XY), F32),
            pltpu.VMEM((3, 8, XY), F32),
            pltpu.VMEM((8, XY), F32),
            pltpu.VMEM((3, 8, XY), F32),
            pltpu.VMEM((VIEWS, XY, lanes), BF16),
            pltpu.VMEM((VIEWS, XY, lanes), BF16),
            pltpu.VMEM((VIEWS, lanes, XY), BF16),
            pltpu.VMEM((VIEWS, lanes, XY), BF16),
            pltpu.VMEM((VIEWS, 2 * SZ, ROWS), BF16),
            pltpu.VMEM((2 * WIDE, VIEWS * SZ), BF16),
            pltpu.VMEM((VIEWS, SZ, XY), F32),
            pltpu.VMEM((VIEWS, 2 * SZ, XY), BF16),
            pltpu.VMEM((VIEWS * SZ, group), BF16),
            pltpu.VMEM((VIEWS * SZ, group), BF16),
            pltpu.VMEM((WIDE, lanes), F32),
            pltpu.VMEM((2, WIDE, XY), F32),
            pltpu.VMEM((2, xslots, WIDE, XY), F32),
            pltpu.VMEM((2, 16, XY), F32),
            pltpu.VMEM((SZ, XY), F32),
            pltpu.SemaphoreType.DMA((SEMAPHORES,)),
            pltpu.SemaphoreType.DMA((SEMAPHORES,)),
        ],
        compiler_params=pltpu.CompilerParams(
            collective_id=0, has_side_effects=True, vmem_limit_bytes=56 * 1024 * 1024
        ),
    )(
        estimate, raw_views, psf, psf, offsets.T,
        coverage.transpose(1, 2, 3, 0).reshape(1, VIEWS),
    )


def solution(mesh):
    counts = (mesh.shape["bx"], mesh.shape["by"], mesh.shape["bz"])
    return jax.shard_map(
        functools.partial(on_device, counts),
        mesh=mesh,
        in_specs=(
            P("bx", "by", "bz"),
            P(None, "bx", "by", "bz"),
            P(),
            P(),
            P(None, "bx", "by", "bz"),
        ),
        out_specs=P("bx", "by", "bz"),
        check_vma=False,
    )
```

```python
import functools

import jax
import jax.numpy as jnp
from jax import lax
from jax.experimental import pallas as pl
from jax.experimental.pallas import tpu as pltpu
from jax.sharding import PartitionSpec as P

F32 = jnp.float32
BF16 = jnp.bfloat16
MESH = pl.DeviceIdType.MESH
OFF = 8
TAPS = 31
REACH = 15
VIEWS = 6
SEMAPHORES = 48
SX = 16
SY = 16
SZ = 128
XY = SX * SY
LOW, HIGH, WIDE, ROWS = 16, SZ + 16, SZ + 32, 256


def split(value):
    high = value.astype(BF16)
    return high, (value - high.astype(F32)).astype(BF16)


def dot(a, b):
    return jnp.dot(a, b, preferred_element_type=F32)


def iota(shape, dim):
    return lax.broadcasted_iota(jnp.int32, shape, dim)


def dot3(stack, b_high, b_low):
    half = stack.shape[0] // 2
    both = dot(stack, b_high)
    return both[:half] + (both[half:] + dot(stack[:half], b_low))


def kernel(
    counts, est, raw, psf_v, offsets, coverage, out,
    wide, wide_h, wide_l, cov, rx_a, rx_b, ry_a, ry_b, rz_a, rz_b, kn, knz, patterns,
    kron_h, kron_l, kront_h, kront_l, fz, bz,
    blurred, ratio, back_h, back_l, spread, from_x, from_y, from_z, weights, send, recv,
):
    nx, ny, nz = counts
    xslots = 2 if nx == 2 else 3
    group = 3 * XY
    lanes = xslots * group
    ix, iy, iz = lax.axis_index("bx"), lax.axis_index("by"), lax.axis_index("bz")
    where = {"bx": (ix, nx), "by": (iy, ny), "bz": (iz, nz)}
    has_left = {name: i > 0 for name, (i, n) in where.items()}
    has_right = {name: i < n - 1 for name, (i, n) in where.items()}
    x_shift = [0, 1 - 2 * ix] if nx == 2 else [0, -1, 1]
    y_shift = [0, -1, 1]
    x_left_slot = 1
    x_right_slot = 1 if nx == 2 else 2
    used = iter(range(SEMAPHORES))

    def to_side(axis, left, src, dst):
        index = next(used)
        return axis, left, pltpu.make_async_remote_copy(
            src_ref=src, dst_ref=dst, send_sem=send.at[index], recv_sem=recv.at[index],
            device_id={axis: where[axis][0] + (-1 if left else 1)}, device_id_type=MESH,
        )

    def to_left(axis, src, dst):
        return to_side(axis, True, src, dst)

    def to_right(axis, src, dst):
        return to_side(axis, False, src, dst)

    def start(copies):
        for axis, left, copy in copies:
            @pl.when(has_left[axis] if left else has_right[axis])
            def _():
                copy.start()

    def arrive(copies):
        for axis, left, copy in copies:
            @pl.when(has_right[axis] if left else has_left[axis])
            def _():
                copy.wait_recv()

    def sent(copies):
        for axis, left, copy in copies:
            @pl.when(has_left[axis] if left else has_right[axis])
            def _():
                copy.wait_send()

    def absent(axis, left, ref, index):
        @pl.when(jnp.logical_not(has_left[axis] if left else has_right[axis]))
        def _():
            ref[index] = jnp.zeros(ref.at[index].shape, ref.dtype)

    def block(x, y):
        return slice((3 * x + y) * XY, (3 * x + y + 1) * XY)

    full = slice(None)
    own = slice(LOW, HIGH)

    barrier = pltpu.get_barrier_semaphore()
    for axis, (i, n) in where.items():
        @pl.when(has_left[axis])
        def _():
            pl.semaphore_signal(barrier, inc=1, device_id={axis: i - 1}, device_id_type=MESH)

        @pl.when(has_right[axis])
        def _():
            pl.semaphore_signal(barrier, inc=1, device_id={axis: i + 1}, device_id_type=MESH)

    wide[own, block(0, 0)] = est[...].reshape(XY, SZ).T
    cov_rows = jnp.zeros((8, SZ), F32)
    for view in range(VIEWS):
        value = coverage[0, view].astype(F32)
        cov_rows = jnp.where(iota((8, SZ), 0) == view, value, cov_rows)
    cov[0, 0, 1] = cov_rows

    degree = sum(
        (has_left[axis].astype(jnp.int32) + has_right[axis].astype(jnp.int32) for axis in where),
        jnp.int32(0),
    )
    pl.semaphore_wait(barrier, degree)

    half = VIEWS // 2
    first, last = slice(0, half), slice(half, VIEWS)
    est_z = [
        to_left("bz", wide.at[LOW : LOW + 16, block(0, 0)], wide.at[HIGH:WIDE, block(0, 0)]),
        to_right("bz", wide.at[HIGH - 16 : HIGH, block(0, 0)], wide.at[0:LOW, block(0, 0)]),
        to_left("bz", cov.at[0, 0, 1], cov.at[0, 0, 2]),
        to_right("bz", cov.at[0, 0, 1], cov.at[0, 0, 0]),
    ]
    est_x = [
        to_left("bx", wide.at[:, block(0, 0)], wide.at[:, block(x_right_slot, 0)]),
        to_right("bx", wide.at[:, block(0, 0)], wide.at[:, block(x_left_slot, 0)]),
        to_left("bx", cov.at[0, 0], cov.at[0, x_right_slot]),
        to_right("bx", cov.at[0, 0], cov.at[0, x_left_slot]),
    ]
    est_y = [
        [
            to_left("by", wide.at[:, block(x, 0)], wide.at[:, block(x, 2)]),
            to_right("by", wide.at[:, block(x, 0)], wide.at[:, block(x, 1)]),
        ]
        for x in range(xslots)
    ]
    cov_y = [
        to_left("by", cov.at[0], cov.at[2]),
        to_right("by", cov.at[0], cov.at[1]),
    ]
    raw_ax = [
        to_left("bx", raw.at[first, 0:8], rx_a.at[:, 24:32]),
        to_right("bx", raw.at[first, 8:16], rx_a.at[:, 0:8]),
    ]
    raw_ay = [
        to_left("by", ry_a.at[:, :, 8:16], ry_a.at[:, :, 24:32]),
        to_right("by", ry_a.at[:, :, 16:24], ry_a.at[:, :, 0:8]),
    ]
    raw_by = [
        to_left("by", raw.at[last, :, 0:8], ry_b.at[:, :, 24:32]),
        to_right("by", raw.at[last, :, 8:16], ry_b.at[:, :, 0:8]),
    ]
    raw_bx = [
        to_left("bx", rx_b.at[:, 8:16], rx_b.at[:, 24:32]),
        to_right("bx", rx_b.at[:, 16:24], rx_b.at[:, 0:8]),
    ]
    raw_az, raw_bz = [
        [
            to_left("bz", rz.at[:, 8:16], rz.at[:, 136:144]),
            to_right("bz", rz.at[:, 128:136], rz.at[:, 0:8]),
        ]
        for rz in (rz_a, rz_b)
    ]

    start(est_z)
    start(raw_ax)
    start(raw_by)

    blank = jnp.zeros((ROWS - WIDE, lanes), BF16)
    wide_h[WIDE:ROWS, :] = blank
    wide_l[WIDE:ROWS, :] = blank
    if nx > 2:
        for left, slot in ((True, x_left_slot), (False, x_right_slot)):
            absent("bx", left, wide, (full, block(slot, 0)))
            absent("bx", left, cov, (0, slot, full, full, full))
    for left, slot in ((True, 1), (False, 2)):
        for x in range(xslots):
            absent("by", left, wide, (full, block(x, slot)))
        absent("by", left, cov, (slot, full, full, full, full))
    absent("bz", True, wide, (slice(0, LOW), block(0, 0)))
    absent("bz", False, wide, (slice(HIGH, WIDE), block(0, 0)))
    absent("bz", True, cov, (0, 0, 0, full, full))
    absent("bz", False, cov, (0, 0, 2, full, full))
    for rx, ry in ((rx_a, ry_a), (rx_b, ry_b)):
        absent("bx", True, rx, (full, slice(0, 8), full, full))
        absent("bx", False, rx, (full, slice(24, 32), full, full))
        absent("by", True, ry, (full, full, slice(0, 8), full))
        absent("by", False, ry, (full, full, slice(24, 32), full))
    for rz in (rz_a, rz_b):
        absent("bz", True, rz, (full, slice(0, 8), full))
        absent("bz", False, rz, (full, slice(136, 144), full))
    absent("bz", True, from_z, (0, full, full))
    absent("bz", False, from_z, (1, full, full))
    absent("by", True, from_y, (0, full, full, full))
    absent("by", False, from_y, (1, full, full, full))
    absent("bx", True, from_x, (0, full, full))
    absent("bx", False, from_x, (1, full, full))
    rx_a[:, 8:24] = raw[first]
    ry_b[:, :, 8:24] = raw[last]

    kn[...] = jnp.zeros(kn.shape, F32)
    for axis in range(3):
        values = psf_v[:, axis, :]
        kn[axis, 0:VIEWS, 0:TAPS] = values / jnp.sum(values, axis=1, keepdims=True)
    knz[...] = pltpu.roll(kn[2], 1, 1)

    highest = lax.Precision.HIGHEST
    row, lane = iota((XY, XY), 0), iota((XY, XY), 1)
    lane_x, lane_y = lane // SY, lane % SY
    mirror = (row + lane == TAPS - 1).astype(F32)
    kinds = []
    for flip in (False, True):
        for axis, cell, shifts, size in ((0, lane_x, x_shift, SX), (1, lane_y, y_shift, SY)):
            taps = kn[axis]
            if flip:
                taps = jnp.dot(taps, mirror, precision=highest, preferred_element_type=F32)
            taps = pltpu.roll(taps, XY - REACH, 1)
            bands = [
                pltpu.roll(
                    jnp.broadcast_to(taps[view : view + 1, :], (16, XY)), 0, 1, stride=1, stride_axis=0
                )
                for view in range(VIEWS)
            ]
            stack = jnp.concatenate(split(jnp.concatenate(bands, axis=0)), axis=0)
            for shift in shifts:
                place = cell + (-size if flip else size) * shift
                chosen = (row == jnp.where(place < 0, place + XY, place)).astype(BF16)
                both = dot(stack, chosen)
                patterns[len(kinds)] = both[: 16 * VIEWS] + both[16 * VIEWS :]
                kinds.append((flip, axis, shift))
    blur_x, blur_y = 0, xslots
    turn_x, turn_y = xslots + 3, 2 * xslots + 3

    arrive(est_z)
    start(est_x)
    start(est_y[0])

    @pl.loop(0, VIEWS)
    def _(view):
        rows_of = pl.ds(pl.multiple_of(view * 16, 16), 16)
        for x in range(xslots):
            to_x, from_x_row = patterns[blur_x + x, rows_of, :], patterns[turn_x + x, rows_of, :]
            for y in range(3):
                to_y, from_y_row = patterns[blur_y + y, rows_of, :], patterns[turn_y + y, rows_of, :]
                base = (3 * x + y) * XY
                for i in range(16):
                    high, low = split(to_y * to_x[i : i + 1, :])
                    kron_h[view, i * 16 : (i + 1) * 16, base : base + XY] = high
                    kron_l[view, i * 16 : (i + 1) * 16, base : base + XY] = low
                    high, low = split(from_y_row * from_x_row[i : i + 1, :])
                    kront_h[view, base + i * 16 : base + (i + 1) * 16, :] = high
                    kront_l[view, base + i * 16 : base + (i + 1) * 16, :] = low
        line = jnp.broadcast_to(knz[pl.ds(view, 1), :], (SZ, ROWS))
        band = pltpu.roll(line, 0, 1, stride=1, stride_axis=0)
        fz[view, 0:SZ], fz[view, SZ : 2 * SZ] = split(band)
        columns = pl.ds(pl.multiple_of(view * SZ, SZ), SZ)
        bz[0:WIDE, columns], bz[WIDE : 2 * WIDE, columns] = split(band.T[0:WIDE])

    def forward(x, begin, end):
        cut = slice((3 * x + begin) * XY, (3 * x + end) * XY)
        wide_h[0:WIDE, cut], wide_l[0:WIDE, cut] = split(wide[:, cut])

        @pl.loop(0, VIEWS, step=2)
        def _(pair):
            for view in (pair, pair + 1):
                part = dot3(fz[view], wide_h[:, cut], wide_l[:, cut])
                stack = jnp.concatenate(split(part), axis=0)
                part = dot3(stack, kront_h[view, cut, :], kront_l[view, cut, :])
                if x == 0 and begin == 0:
                    blurred[view] = part
                else:
                    blurred[view] = blurred[view] + part

    def turned_y(ry, view, offset):
        return pltpu.roll(ry[view], lax.rem(32 - OFF - offset, 32), 1)[:, 0:SY, :]

    arrive(raw_by)

    @pl.loop(0, half)
    def _(view):
        rx_b[view, 8:24] = turned_y(ry_b, view, offsets[1, half + view])

    start(raw_bx)
    arrive(raw_ax)

    @pl.loop(0, half)
    def _(view):
        ry_a[view, :, 8:24, :] = rx_a[view, pl.ds(OFF + offsets[0, view], SX), :, :]

    start(raw_ay)
    forward(0, 0, 1)
    arrive(est_x)
    for x in range(1, xslots):
        start(est_y[x])
    start(cov_y)
    for x in range(1, xslots):
        forward(x, 0, 1)
    arrive(est_y[0])
    forward(0, 1, 3)
    arrive(raw_bx)

    @pl.loop(0, half)
    def _(view):
        shifted = rx_b[view, pl.ds(OFF + offsets[0, half + view], SX), :, :]
        rz_b[view, 8:136, :] = shifted.reshape(XY, SZ).T

    start(raw_bz)
    for x in range(1, xslots):
        arrive(est_y[x])
        forward(x, 1, 3)
    arrive(raw_ay)

    @pl.loop(0, half)
    def _(view):
        rz_a[view, 8:136, :] = turned_y(ry_a, view, offsets[1, view]).reshape(XY, SZ).T

    start(raw_az)

    def make_ratio(rz, base):
        @pl.loop(0, half)
        def _(index):
            view = base + index
            turn = lax.rem(SZ + 16 - OFF - offsets[2, view], SZ + 16)
            observed = pltpu.roll(rz[index], turn, 0)[0:SZ, :]
            mask = coverage[0, view].astype(F32)
            value = mask * observed / blurred[view]
            ratio[view, 0:SZ], ratio[view, SZ : 2 * SZ] = split(value)

    def backward(x, views):
        cut = slice(x * group, (x + 1) * group)
        for view in views:
            part = dot3(ratio[view], kron_h[view, :, cut], kron_l[view, :, cut])
            rows_of = slice(view * SZ, (view + 1) * SZ)
            back_h[rows_of, cut], back_l[rows_of, cut] = split(part)

    arrive(raw_bz)
    make_ratio(rz_b, half)
    for x in range(xslots):
        backward(x, range(half, VIEWS))
    arrive(raw_az)
    make_ratio(rz_a, 0)

    back_y = [
        [
            to_left("by", spread.at[:, block(x, 1)], from_y.at[1, x]),
            to_right("by", spread.at[:, block(x, 2)], from_y.at[0, x]),
        ]
        for x in range(xslots)
    ]
    back_x = [
        to_left("bx", spread.at[:, block(x_left_slot, 0)], from_x.at[1]),
        to_right("bx", spread.at[:, block(x_right_slot, 0)], from_x.at[0]),
    ]
    back_z = [
        to_left("bz", spread.at[0:LOW, block(0, 0)], from_z.at[1]),
        to_right("bz", spread.at[HIGH:WIDE, block(0, 0)], from_z.at[0]),
    ]

    def add_y(x):
        arrive(back_y[x])
        spread[:, block(x, 0)] = spread[:, block(x, 0)] + (from_y[0, x] + from_y[1, x])

    for x in reversed(range(xslots)):
        backward(x, range(half))
        for y in (1, 2, 0):
            spread[:, block(x, y)] = dot3(bz[...], back_h[:, block(x, y)], back_l[:, block(x, y)])
            if y > 0:
                start(back_y[x][y - 1 : y])
    for x in range(1, xslots):
        add_y(x)
    start(back_x)

    arrive(cov_y)

    def factor(axis, position, shift, size):
        cell = position + REACH - row[:, : position.shape[1]] - shift * size
        inside = ((cell >= 0) & (cell < size)).astype(F32)
        return jnp.dot(kn[axis], inside, precision=highest, preferred_element_type=F32)

    factor_x = [factor(0, lane_x, d, SX) for d in x_shift]
    factor_y = [factor(1, lane_y, d, SY) for d in y_shift]
    factor_z = [factor(2, lane[:, :SZ], d, SZ) for d in (-1, 0, 1)]
    rows = []
    for z in range(3):
        total = jnp.zeros((8, XY), F32)
        for y in range(3):
            part = jnp.zeros((8, XY), F32)
            for x in range(xslots):
                part = part + jnp.concatenate([cov[y, x, z]] * 2, axis=1) * factor_x[x]
            total = total + part * factor_y[y]
        rows.append(total)
    weights[...] = jnp.dot(
        jnp.concatenate(factor_z, axis=0).T, jnp.concatenate(rows, axis=0),
        precision=highest, preferred_element_type=F32,
    )

    add_y(0)
    arrive(back_x)
    spread[:, block(0, 0)] = spread[:, block(0, 0)] + (from_x[0] + from_x[1])
    start(back_z)
    arrive(back_z)
    total = spread[own, block(0, 0)]
    total = jnp.concatenate(
        [total[0:16] + from_z[0], total[16 : SZ - 16], total[SZ - 16 : SZ] + from_z[1]], axis=0
    )
    restored = wide[own, block(0, 0)] * total / weights[...]
    out[...] = restored.T.reshape(SX, SY, SZ)
    for copies in [est_x, *est_y, cov_y, est_z, raw_ax, raw_ay, raw_bx, raw_by, raw_az, raw_bz]:
        sent(copies)
    for copies in [*back_y, back_x, back_z]:
        sent(copies)


def on_device(counts, estimate, raw_views, psf, offsets, coverage):
    xslots = 2 if counts[0] == 2 else 3
    group = 3 * XY
    lanes = xslots * group
    vmem = pl.BlockSpec(memory_space=pltpu.VMEM)
    smem = pl.BlockSpec(memory_space=pltpu.SMEM)
    return pl.pallas_call(
        functools.partial(kernel, counts),
        out_shape=jax.ShapeDtypeStruct(estimate.shape, F32),
        in_specs=[vmem, vmem, vmem, smem, smem],
        out_specs=vmem,
        scratch_shapes=[
            pltpu.VMEM((WIDE, lanes), F32),
            pltpu.VMEM((ROWS, lanes), BF16),
            pltpu.VMEM((ROWS, lanes), BF16),
            pltpu.VMEM((3, xslots, 3, 8, SZ), F32),
            pltpu.VMEM((VIEWS // 2, 32, SY, SZ), F32),
            pltpu.VMEM((VIEWS // 2, 32, SY, SZ), F32),
            pltpu.VMEM((VIEWS // 2, SX, 32, SZ), F32),
            pltpu.VMEM((VIEWS // 2, SX, 32, SZ), F32),
            pltpu.VMEM((VIEWS // 2, SZ + 16, XY), F32),
            pltpu.VMEM((VIEWS // 2, SZ + 16, XY), F32),
            pltpu.VMEM((3, 8, XY), F32),
            pltpu.VMEM((8, XY), F32),
            pltpu.VMEM((2 * xslots + 6, 16 * VIEWS, XY), F32),
            pltpu.VMEM((VIEWS, XY, lanes), BF16),
            pltpu.VMEM((VIEWS, XY, lanes), BF16),
            pltpu.VMEM((VIEWS, lanes, XY), BF16),
            pltpu.VMEM((VIEWS, lanes, XY), BF16),
            pltpu.VMEM((VIEWS, 2 * SZ, ROWS), BF16),
            pltpu.VMEM((2 * WIDE, VIEWS * SZ), BF16),
            pltpu.VMEM((VIEWS, SZ, XY), F32),
            pltpu.VMEM((VIEWS, 2 * SZ, XY), BF16),
            pltpu.VMEM((VIEWS * SZ, lanes), BF16),
            pltpu.VMEM((VIEWS * SZ, lanes), BF16),
            pltpu.VMEM((WIDE, lanes), F32),
            pltpu.VMEM((2, WIDE, XY), F32),
            pltpu.VMEM((2, xslots, WIDE, XY), F32),
            pltpu.VMEM((2, 16, XY), F32),
            pltpu.VMEM((SZ, XY), F32),
            pltpu.SemaphoreType.DMA((SEMAPHORES,)),
            pltpu.SemaphoreType.DMA((SEMAPHORES,)),
        ],
        compiler_params=pltpu.CompilerParams(
            collective_id=0, has_side_effects=True, vmem_limit_bytes=56 * 1024 * 1024
        ),
    )(
        estimate, raw_views, psf, offsets.T,
        coverage.transpose(1, 2, 3, 0).reshape(1, VIEWS),
    )


def solution(mesh):
    counts = (mesh.shape["bx"], mesh.shape["by"], mesh.shape["bz"])
    return jax.shard_map(
        functools.partial(on_device, counts),
        mesh=mesh,
        in_specs=(
            P("bx", "by", "bz"),
            P(None, "bx", "by", "bz"),
            P(),
            P(),
            P(None, "bx", "by", "bz"),
        ),
        out_specs=P("bx", "by", "bz"),
        check_vma=False,
    )
```

```python
import functools

import jax
import jax.numpy as jnp
from jax import lax
from jax.experimental import pallas as pl
from jax.experimental.pallas import tpu as pltpu
from jax.sharding import PartitionSpec as P

F32 = jnp.float32
BF16 = jnp.bfloat16
MESH = pl.DeviceIdType.MESH
OFF = 8
TAPS = 31
REACH = 15
VIEWS = 6
SEMAPHORES = 48
SX = 16
SY = 16
SZ = 128
XY = SX * SY
LOW, HIGH, WIDE, ROWS = 16, SZ + 16, SZ + 32, 256


def split(value):
    high = value.astype(BF16)
    return high, (value - high.astype(F32)).astype(BF16)


def dot(a, b):
    return jnp.dot(a, b, preferred_element_type=F32)


def iota(shape, dim):
    return lax.broadcasted_iota(jnp.int32, shape, dim)


def dot3(stack, b_high, b_low):
    half = stack.shape[0] // 2
    both = dot(stack, b_high)
    return both[:half] + (both[half:] + dot(stack[:half], b_low))


def kernel(
    counts, est, raw, psf_v, offsets, coverage, out,
    wide, wide_s, cov, rx_a, rx_b, ry_a, ry_b, rz_a, rz_b, kn, knz, patterns,
    kron_h, kron_l, kront_h, kront_l, fz, bz,
    blurred, back, spread, from_x, from_y, from_z, weights, send, recv,
):
    nx, ny, nz = counts
    xslots = 2 if nx == 2 else 3
    group = 3 * XY
    lanes = xslots * group
    ix, iy, iz = lax.axis_index("bx"), lax.axis_index("by"), lax.axis_index("bz")
    where = {"bx": (ix, nx), "by": (iy, ny), "bz": (iz, nz)}
    has_left = {name: i > 0 for name, (i, n) in where.items()}
    has_right = {name: i < n - 1 for name, (i, n) in where.items()}
    x_shift = [0, 1 - 2 * ix] if nx == 2 else [0, -1, 1]
    y_shift = [0, -1, 1]
    x_left_slot = 1
    x_right_slot = 1 if nx == 2 else 2
    used = iter(range(SEMAPHORES))

    def to_side(axis, left, src, dst):
        index = next(used)
        return axis, left, pltpu.make_async_remote_copy(
            src_ref=src, dst_ref=dst, send_sem=send.at[index], recv_sem=recv.at[index],
            device_id={axis: where[axis][0] + (-1 if left else 1)}, device_id_type=MESH,
        )

    def to_left(axis, src, dst):
        return to_side(axis, True, src, dst)

    def to_right(axis, src, dst):
        return to_side(axis, False, src, dst)

    def start(copies):
        for axis, left, copy in copies:
            @pl.when(has_left[axis] if left else has_right[axis])
            def _():
                copy.start()

    def arrive(copies):
        for axis, left, copy in copies:
            @pl.when(has_right[axis] if left else has_left[axis])
            def _():
                copy.wait_recv()

    def sent(copies):
        for axis, left, copy in copies:
            @pl.when(has_left[axis] if left else has_right[axis])
            def _():
                copy.wait_send()

    def absent(axis, left, ref, index):
        @pl.when(jnp.logical_not(has_left[axis] if left else has_right[axis]))
        def _():
            ref[index] = jnp.zeros(ref.at[index].shape, ref.dtype)

    def block(x, y):
        return slice((3 * x + y) * XY, (3 * x + y + 1) * XY)

    full = slice(None)
    own = slice(LOW, HIGH)

    barrier = pltpu.get_barrier_semaphore()
    for axis, (i, n) in where.items():
        @pl.when(has_left[axis])
        def _():
            pl.semaphore_signal(barrier, inc=1, device_id={axis: i - 1}, device_id_type=MESH)

        @pl.when(has_right[axis])
        def _():
            pl.semaphore_signal(barrier, inc=1, device_id={axis: i + 1}, device_id_type=MESH)

    wide[own, block(0, 0)] = est[...].reshape(XY, SZ).T
    cov_rows = jnp.zeros((8, SZ), F32)
    for view in range(VIEWS):
        value = coverage[0, view].astype(F32)
        cov_rows = jnp.where(iota((8, SZ), 0) == view, value, cov_rows)
    cov[0, 0, 1] = cov_rows

    degree = sum(
        (has_left[axis].astype(jnp.int32) + has_right[axis].astype(jnp.int32) for axis in where),
        jnp.int32(0),
    )
    pl.semaphore_wait(barrier, degree)

    half = VIEWS // 2
    first, last = slice(0, half), slice(half, VIEWS)
    est_z = [
        to_left("bz", wide.at[LOW : LOW + 16, block(0, 0)], wide.at[HIGH:WIDE, block(0, 0)]),
        to_right("bz", wide.at[HIGH - 16 : HIGH, block(0, 0)], wide.at[0:LOW, block(0, 0)]),
        to_left("bz", cov.at[0, 0, 1], cov.at[0, 0, 2]),
        to_right("bz", cov.at[0, 0, 1], cov.at[0, 0, 0]),
    ]
    est_x = [
        to_left("bx", wide.at[:, block(0, 0)], wide.at[:, block(x_right_slot, 0)]),
        to_right("bx", wide.at[:, block(0, 0)], wide.at[:, block(x_left_slot, 0)]),
        to_left("bx", cov.at[0, 0], cov.at[0, x_right_slot]),
        to_right("bx", cov.at[0, 0], cov.at[0, x_left_slot]),
    ]
    est_y = [
        [
            to_left("by", wide.at[:, block(x, 0)], wide.at[:, block(x, 2)]),
            to_right("by", wide.at[:, block(x, 0)], wide.at[:, block(x, 1)]),
        ]
        for x in range(xslots)
    ]
    cov_y = [
        to_left("by", cov.at[0], cov.at[2]),
        to_right("by", cov.at[0], cov.at[1]),
    ]
    raw_ax = [
        to_left("bx", raw.at[first, 0:8], rx_a.at[:, 24:32]),
        to_right("bx", raw.at[first, 8:16], rx_a.at[:, 0:8]),
    ]
    raw_ay = [
        to_left("by", ry_a.at[:, :, 8:16], ry_a.at[:, :, 24:32]),
        to_right("by", ry_a.at[:, :, 16:24], ry_a.at[:, :, 0:8]),
    ]
    raw_by = [
        to_left("by", raw.at[last, :, 0:8], ry_b.at[:, :, 24:32]),
        to_right("by", raw.at[last, :, 8:16], ry_b.at[:, :, 0:8]),
    ]
    raw_bx = [
        to_left("bx", rx_b.at[:, 8:16], rx_b.at[:, 24:32]),
        to_right("bx", rx_b.at[:, 16:24], rx_b.at[:, 0:8]),
    ]
    raw_az, raw_bz = [
        [
            to_left("bz", rz.at[:, 8:16], rz.at[:, 136:144]),
            to_right("bz", rz.at[:, 128:136], rz.at[:, 0:8]),
        ]
        for rz in (rz_a, rz_b)
    ]

    start(est_z)
    start(raw_ax)
    start(raw_by)

    if nx > 2:
        for left, slot in ((True, x_left_slot), (False, x_right_slot)):
            absent("bx", left, wide, (full, block(slot, 0)))
            absent("bx", left, cov, (0, slot, full, full, full))
    for left, slot in ((True, 1), (False, 2)):
        for x in range(xslots):
            absent("by", left, wide, (full, block(x, slot)))
        absent("by", left, cov, (slot, full, full, full, full))
    absent("bz", True, wide, (slice(0, LOW), block(0, 0)))
    absent("bz", False, wide, (slice(HIGH, WIDE), block(0, 0)))
    absent("bz", True, cov, (0, 0, 0, full, full))
    absent("bz", False, cov, (0, 0, 2, full, full))
    for rx, ry in ((rx_a, ry_a), (rx_b, ry_b)):
        absent("bx", True, rx, (full, slice(0, 8), full, full))
        absent("bx", False, rx, (full, slice(24, 32), full, full))
        absent("by", True, ry, (full, full, slice(0, 8), full))
        absent("by", False, ry, (full, full, slice(24, 32), full))
    for rz in (rz_a, rz_b):
        absent("bz", True, rz, (full, slice(0, 8), full))
        absent("bz", False, rz, (full, slice(136, 144), full))
    absent("bz", True, from_z, (0, full, full))
    absent("bz", False, from_z, (1, full, full))
    absent("by", True, from_y, (0, full, full, full))
    absent("by", False, from_y, (1, full, full, full))
    absent("bx", True, from_x, (0, full, full))
    absent("bx", False, from_x, (1, full, full))
    rx_a[:, 8:24] = raw[first]
    ry_b[:, :, 8:24] = raw[last]

    kn[...] = jnp.zeros(kn.shape, F32)
    for axis in range(3):
        values = psf_v[:, axis, :]
        kn[axis, 0:VIEWS, 0:TAPS] = values / jnp.sum(values, axis=1, keepdims=True)
    knz[...] = pltpu.roll(kn[2], 1, 1)

    highest = lax.Precision.HIGHEST
    row, lane = iota((XY, XY), 0), iota((XY, XY), 1)
    lane_x, lane_y = lane // SY, lane % SY
    mirror = (row + lane == TAPS - 1).astype(F32)
    kinds = []
    for flip in (False, True):
        for axis, cell, shifts, size in ((0, lane_x, x_shift, SX), (1, lane_y, y_shift, SY)):
            taps = kn[axis]
            if flip:
                taps = jnp.dot(taps, mirror, precision=highest, preferred_element_type=F32)
            taps = pltpu.roll(taps, XY - REACH, 1)
            bands = [
                pltpu.roll(
                    jnp.broadcast_to(taps[view : view + 1, :], (16, XY)), 0, 1, stride=1, stride_axis=0
                )
                for view in range(VIEWS)
            ]
            stack = jnp.concatenate(split(jnp.concatenate(bands, axis=0)), axis=0)
            for shift in shifts:
                place = cell + (-size if flip else size) * shift
                chosen = (row == jnp.where(place < 0, place + XY, place)).astype(BF16)
                both = dot(stack, chosen)
                patterns[len(kinds)] = both[: 16 * VIEWS] + both[16 * VIEWS :]
                kinds.append((flip, axis, shift))
    blur_x, blur_y = 0, xslots
    turn_x, turn_y = xslots + 3, 2 * xslots + 3

    arrive(est_z)
    start(est_x)
    start(est_y[0])

    def rows_of(view, i):
        return pl.ds(pl.multiple_of(view * XY + i * 16, 16), 16)

    def pattern(kind, view):
        return patterns[kind, pl.ds(pl.multiple_of(view * 16, 16), 16), :]

    @pl.loop(0, VIEWS)
    def _(view):
        for x in range(xslots):
            to_x = pattern(turn_x + x, view)
            for y in range(3):
                to_y = pattern(turn_y + y, view)
                base = (3 * x + y) * XY
                for i in range(16):
                    high, low = split(to_y * to_x[i : i + 1, :])
                    kront_h[view, base + i * 16 : base + (i + 1) * 16, :] = high
                    kront_l[view, base + i * 16 : base + (i + 1) * 16, :] = low
        line = jnp.broadcast_to(knz[pl.ds(view, 1), :], (SZ, ROWS))
        band = pltpu.roll(line, 0, 1, stride=1, stride_axis=0)
        fz[view, 0:SZ], fz[view, SZ : 2 * SZ] = split(band)
        bz[view, 0:WIDE], bz[view, WIDE : 2 * WIDE] = split(band.T[0:WIDE])

    def build_adjoint():
        @pl.loop(0, VIEWS)
        def _(view):
            for x in range(xslots):
                to_x = pattern(blur_x + x, view)
                for y in range(3):
                    to_y = pattern(blur_y + y, view)
                    for i in range(16):
                        high, low = split(to_y * to_x[i : i + 1, :])
                        kron_h[rows_of(view, i), block(x, y)] = high
                        kron_l[rows_of(view, i), block(x, y)] = low

    def forward(x, begin, end):
        cut = slice((3 * x + begin) * XY, (3 * x + end) * XY)
        wide_s[0:WIDE, cut], wide_s[WIDE : 2 * WIDE, cut] = split(wide[:, cut])

        @pl.loop(0, VIEWS, step=2)
        def _(pair):
            for view in (pair, pair + 1):
                part = dot3(wide_s[:, cut], kront_h[view, cut, :], kront_l[view, cut, :])
                if x == 0 and begin == 0:
                    blurred[view] = part
                else:
                    blurred[view] = blurred[view] + part

    def turned_y(ry, view, offset):
        return pltpu.roll(ry[view], lax.rem(32 - OFF - offset, 32), 1)[:, 0:SY, :]

    arrive(raw_by)

    @pl.loop(0, half)
    def _(view):
        rx_b[view, 8:24] = turned_y(ry_b, view, offsets[1, half + view])

    start(raw_bx)
    arrive(raw_ax)

    @pl.loop(0, half)
    def _(view):
        ry_a[view, :, 8:24, :] = rx_a[view, pl.ds(OFF + offsets[0, view], SX), :, :]

    start(raw_ay)
    forward(0, 0, 1)
    arrive(est_x)
    for x in range(1, xslots):
        start(est_y[x])
    start(cov_y)
    for x in range(1, xslots):
        forward(x, 0, 1)
    arrive(est_y[0])
    forward(0, 1, 3)
    build_adjoint()
    arrive(raw_bx)

    @pl.loop(0, half)
    def _(view):
        shifted = rx_b[view, pl.ds(OFF + offsets[0, half + view], SX), :, :]
        rz_b[view, 8:136, :] = shifted.reshape(XY, SZ).T

    start(raw_bz)
    for x in range(1, xslots):
        arrive(est_y[x])
        forward(x, 1, 3)
    arrive(raw_ay)

    @pl.loop(0, half)
    def _(view):
        rz_a[view, 8:136, :] = turned_y(ry_a, view, offsets[1, view]).reshape(XY, SZ).T

    start(raw_az)

    rest = jnp.zeros((ROWS - WIDE, XY), BF16)

    def ratios(rz, base):
        for index in range(half):
            view = base + index
            turn = lax.rem(SZ + 16 - OFF - offsets[2, view], SZ + 16)
            observed = pltpu.roll(rz[index], turn, 0)[0:SZ, :]
            mask = coverage[0, view].astype(F32)
            high, low = split(blurred[view])
            high = jnp.concatenate([high, rest], axis=0)
            low = jnp.concatenate([low, rest], axis=0)
            high, low = split(mask * observed / dot3(fz[view], high, low))
            columns = slice(view * XY, (view + 1) * XY)
            back[0:WIDE, columns], back[WIDE : 2 * WIDE, columns] = split(dot3(bz[view], high, low))

    arrive(raw_bz)
    ratios(rz_b, half)
    arrive(raw_az)
    ratios(rz_a, 0)

    back_y = [
        [
            to_left("by", spread.at[:, block(x, 1)], from_y.at[1, x]),
            to_right("by", spread.at[:, block(x, 2)], from_y.at[0, x]),
        ]
        for x in range(xslots)
    ]
    back_x = [
        to_left("bx", spread.at[:, block(x_left_slot, 0)], from_x.at[1]),
        to_right("bx", spread.at[:, block(x_right_slot, 0)], from_x.at[0]),
    ]
    back_z = [
        to_left("bz", spread.at[0:LOW, block(0, 0)], from_z.at[1]),
        to_right("bz", spread.at[HIGH:WIDE, block(0, 0)], from_z.at[0]),
    ]

    def add_y(x):
        arrive(back_y[x])
        spread[:, block(x, 0)] = spread[:, block(x, 0)] + (from_y[0, x] + from_y[1, x])

    for x in reversed(range(xslots)):
        for y in (1, 2, 0):
            spread[:, block(x, y)] = dot3(back[...], kron_h[:, block(x, y)], kron_l[:, block(x, y)])
            if y > 0:
                start(back_y[x][y - 1 : y])
    for x in range(1, xslots):
        add_y(x)
    start(back_x)

    arrive(cov_y)

    def factor(axis, position, shift, size):
        cell = position + REACH - row[:, : position.shape[1]] - shift * size
        inside = ((cell >= 0) & (cell < size)).astype(F32)
        return jnp.dot(kn[axis], inside, precision=highest, preferred_element_type=F32)

    factor_x = [factor(0, lane_x, d, SX) for d in x_shift]
    factor_y = [factor(1, lane_y, d, SY) for d in y_shift]
    factor_z = [factor(2, lane[:, :SZ], d, SZ) for d in (-1, 0, 1)]
    rows = []
    for z in range(3):
        total = jnp.zeros((8, XY), F32)
        for y in range(3):
            part = jnp.zeros((8, XY), F32)
            for x in range(xslots):
                part = part + jnp.concatenate([cov[y, x, z]] * 2, axis=1) * factor_x[x]
            total = total + part * factor_y[y]
        rows.append(total)
    weights[...] = jnp.dot(
        jnp.concatenate(factor_z, axis=0).T, jnp.concatenate(rows, axis=0),
        precision=highest, preferred_element_type=F32,
    )

    add_y(0)
    arrive(back_x)
    spread[:, block(0, 0)] = spread[:, block(0, 0)] + (from_x[0] + from_x[1])
    start(back_z)
    arrive(back_z)
    total = spread[own, block(0, 0)]
    total = jnp.concatenate(
        [total[0:16] + from_z[0], total[16 : SZ - 16], total[SZ - 16 : SZ] + from_z[1]], axis=0
    )
    restored = wide[own, block(0, 0)] * total / weights[...]
    out[...] = restored.T.reshape(SX, SY, SZ)
    for copies in [est_x, *est_y, cov_y, est_z, raw_ax, raw_ay, raw_bx, raw_by, raw_az, raw_bz]:
        sent(copies)
    for copies in [*back_y, back_x, back_z]:
        sent(copies)


def on_device(counts, estimate, raw_views, psf, offsets, coverage):
    xslots = 2 if counts[0] == 2 else 3
    group = 3 * XY
    lanes = xslots * group
    vmem = pl.BlockSpec(memory_space=pltpu.VMEM)
    smem = pl.BlockSpec(memory_space=pltpu.SMEM)
    return pl.pallas_call(
        functools.partial(kernel, counts),
        out_shape=jax.ShapeDtypeStruct(estimate.shape, F32),
        in_specs=[vmem, vmem, vmem, smem, smem],
        out_specs=vmem,
        scratch_shapes=[
            pltpu.VMEM((WIDE, lanes), F32),
            pltpu.VMEM((2 * WIDE, lanes), BF16),
            pltpu.VMEM((3, xslots, 3, 8, SZ), F32),
            pltpu.VMEM((VIEWS // 2, 32, SY, SZ), F32),
            pltpu.VMEM((VIEWS // 2, 32, SY, SZ), F32),
            pltpu.VMEM((VIEWS // 2, SX, 32, SZ), F32),
            pltpu.VMEM((VIEWS // 2, SX, 32, SZ), F32),
            pltpu.VMEM((VIEWS // 2, SZ + 16, XY), F32),
            pltpu.VMEM((VIEWS // 2, SZ + 16, XY), F32),
            pltpu.VMEM((3, 8, XY), F32),
            pltpu.VMEM((8, XY), F32),
            pltpu.VMEM((2 * xslots + 6, 16 * VIEWS, XY), F32),
            pltpu.VMEM((VIEWS * XY, lanes), BF16),
            pltpu.VMEM((VIEWS * XY, lanes), BF16),
            pltpu.VMEM((VIEWS, lanes, XY), BF16),
            pltpu.VMEM((VIEWS, lanes, XY), BF16),
            pltpu.VMEM((VIEWS, 2 * SZ, ROWS), BF16),
            pltpu.VMEM((VIEWS, 2 * WIDE, SZ), BF16),
            pltpu.VMEM((VIEWS, WIDE, XY), F32),
            pltpu.VMEM((2 * WIDE, VIEWS * XY), BF16),
            pltpu.VMEM((WIDE, lanes), F32),
            pltpu.VMEM((2, WIDE, XY), F32),
            pltpu.VMEM((2, xslots, WIDE, XY), F32),
            pltpu.VMEM((2, 16, XY), F32),
            pltpu.VMEM((SZ, XY), F32),
            pltpu.SemaphoreType.DMA((SEMAPHORES,)),
            pltpu.SemaphoreType.DMA((SEMAPHORES,)),
        ],
        compiler_params=pltpu.CompilerParams(
            collective_id=0, has_side_effects=True, vmem_limit_bytes=56 * 1024 * 1024
        ),
    )(
        estimate, raw_views, psf, offsets.T,
        coverage.transpose(1, 2, 3, 0).reshape(1, VIEWS),
    )


def solution(mesh):
    counts = (mesh.shape["bx"], mesh.shape["by"], mesh.shape["bz"])
    return jax.shard_map(
        functools.partial(on_device, counts),
        mesh=mesh,
        in_specs=(
            P("bx", "by", "bz"),
            P(None, "bx", "by", "bz"),
            P(),
            P(),
            P(None, "bx", "by", "bz"),
        ),
        out_specs=P("bx", "by", "bz"),
        check_vma=False,
    )
```

```python
import functools

import jax
import jax.numpy as jnp
from jax import lax
from jax.experimental import pallas as pl
from jax.experimental.pallas import tpu as pltpu
from jax.sharding import PartitionSpec as P

F32 = jnp.float32
BF16 = jnp.bfloat16
MESH = pl.DeviceIdType.MESH
OFF = 8
TAPS = 31
REACH = 15
VIEWS = 6
SEMAPHORES = 48
SX = 16
SY = 16
SZ = 128
XY = SX * SY
LOW, HIGH, WIDE, ROWS = 16, SZ + 16, SZ + 32, 256


def split(value):
    high = value.astype(BF16)
    return high, (value - high.astype(F32)).astype(BF16)


def dot(a, b):
    return jnp.dot(a, b, preferred_element_type=F32)


def iota(shape, dim):
    return lax.broadcasted_iota(jnp.int32, shape, dim)


def dot3(stack, b_high, b_low):
    half = stack.shape[0] // 2
    both = dot(stack, b_high)
    return both[:half] + (both[half:] + dot(stack[:half], b_low))


def kernel(
    counts, est, raw, psf_v, offsets, coverage, out,
    wide, wide_s, cov, rx_a, rx_b, ry_a, ry_b, rz_a, rz_b, kn, knz, patterns,
    kron_h, kron_l, kront_h, kront_l, fz, bz,
    blurred, part_a, part_b, back, spread, from_x, from_y, from_za, from_zb, weights, send, recv,
):
    nx, ny, nz = counts
    xslots = 2 if nx == 2 else 3
    group = 3 * XY
    lanes = xslots * group
    ix, iy, iz = lax.axis_index("bx"), lax.axis_index("by"), lax.axis_index("bz")
    where = {"bx": (ix, nx), "by": (iy, ny), "bz": (iz, nz)}
    has_left = {name: i > 0 for name, (i, n) in where.items()}
    has_right = {name: i < n - 1 for name, (i, n) in where.items()}
    x_shift = [0, 1 - 2 * ix] if nx == 2 else [0, -1, 1]
    y_shift = [0, -1, 1]
    x_left_slot = 1
    x_right_slot = 1 if nx == 2 else 2
    used = iter(range(SEMAPHORES))

    def to_side(axis, left, src, dst):
        index = next(used)
        return axis, left, pltpu.make_async_remote_copy(
            src_ref=src, dst_ref=dst, send_sem=send.at[index], recv_sem=recv.at[index],
            device_id={axis: where[axis][0] + (-1 if left else 1)}, device_id_type=MESH,
        )

    def to_left(axis, src, dst):
        return to_side(axis, True, src, dst)

    def to_right(axis, src, dst):
        return to_side(axis, False, src, dst)

    def start(copies):
        for axis, left, copy in copies:
            @pl.when(has_left[axis] if left else has_right[axis])
            def _():
                copy.start()

    def arrive(copies):
        for axis, left, copy in copies:
            @pl.when(has_right[axis] if left else has_left[axis])
            def _():
                copy.wait_recv()

    def sent(copies):
        for axis, left, copy in copies:
            @pl.when(has_left[axis] if left else has_right[axis])
            def _():
                copy.wait_send()

    def absent(axis, left, ref, index):
        @pl.when(jnp.logical_not(has_left[axis] if left else has_right[axis]))
        def _():
            ref[index] = jnp.zeros(ref.at[index].shape, ref.dtype)

    def block(x, y):
        return slice((3 * x + y) * XY, (3 * x + y + 1) * XY)

    full = slice(None)

    barrier = pltpu.get_barrier_semaphore()
    for axis, (i, n) in where.items():
        @pl.when(has_left[axis])
        def _():
            pl.semaphore_signal(barrier, inc=1, device_id={axis: i - 1}, device_id_type=MESH)

        @pl.when(has_right[axis])
        def _():
            pl.semaphore_signal(barrier, inc=1, device_id={axis: i + 1}, device_id_type=MESH)

    wide[:, block(0, 0)] = est[...].reshape(XY, SZ).T
    cov_rows = jnp.zeros((8, SZ), F32)
    for view in range(VIEWS):
        value = coverage[0, view].astype(F32)
        cov_rows = jnp.where(iota((8, SZ), 0) == view, value, cov_rows)
    cov[0, 0, 1] = cov_rows

    degree = sum(
        (has_left[axis].astype(jnp.int32) + has_right[axis].astype(jnp.int32) for axis in where),
        jnp.int32(0),
    )
    pl.semaphore_wait(barrier, degree)

    half = VIEWS // 2
    first, last = slice(0, half), slice(half, VIEWS)
    est_x = [
        to_left("bx", wide.at[:, block(0, 0)], wide.at[:, block(x_right_slot, 0)]),
        to_right("bx", wide.at[:, block(0, 0)], wide.at[:, block(x_left_slot, 0)]),
    ]
    cov_z = [
        to_left("bz", cov.at[0, 0, 1], cov.at[0, 0, 2]),
        to_right("bz", cov.at[0, 0, 1], cov.at[0, 0, 0]),
    ]
    cov_x = [
        to_left("bx", cov.at[0, 0], cov.at[0, x_right_slot]),
        to_right("bx", cov.at[0, 0], cov.at[0, x_left_slot]),
    ]
    est_y = [
        [
            to_left("by", wide.at[:, block(x, 0)], wide.at[:, block(x, 2)]),
            to_right("by", wide.at[:, block(x, 0)], wide.at[:, block(x, 1)]),
        ]
        for x in range(xslots)
    ]
    cov_y = [
        to_left("by", cov.at[0], cov.at[2]),
        to_right("by", cov.at[0], cov.at[1]),
    ]
    raw_ax = [
        to_left("bx", raw.at[first, 0:8], rx_a.at[:, 24:32]),
        to_right("bx", raw.at[first, 8:16], rx_a.at[:, 0:8]),
    ]
    raw_ay = [
        to_left("by", ry_a.at[:, :, 8:16], ry_a.at[:, :, 24:32]),
        to_right("by", ry_a.at[:, :, 16:24], ry_a.at[:, :, 0:8]),
    ]
    raw_by = [
        to_left("by", raw.at[last, :, 0:8], ry_b.at[:, :, 24:32]),
        to_right("by", raw.at[last, :, 8:16], ry_b.at[:, :, 0:8]),
    ]
    raw_bx = [
        to_left("bx", rx_b.at[:, 8:16], rx_b.at[:, 24:32]),
        to_right("bx", rx_b.at[:, 16:24], rx_b.at[:, 0:8]),
    ]
    raw_az, raw_bz = [
        [
            to_left("bz", rz.at[:, 8:16], rz.at[:, 136:144]),
            to_right("bz", rz.at[:, 128:136], rz.at[:, 0:8]),
        ]
        for rz in (rz_a, rz_b)
    ]

    mid_z = [
        to_left("bz", blurred.at[:, LOW : LOW + 16], blurred.at[:, HIGH:WIDE]),
        to_right("bz", blurred.at[:, HIGH - 16 : HIGH], blurred.at[:, 0:LOW]),
    ]

    start(est_x)
    start(est_y[0])
    start(cov_z)
    start(raw_by)
    start(raw_ax)

    if nx > 2:
        for left, slot in ((True, x_left_slot), (False, x_right_slot)):
            absent("bx", left, wide, (full, block(slot, 0)))
            absent("bx", left, cov, (0, slot, full, full, full))
    for left, slot in ((True, 1), (False, 2)):
        for x in range(xslots):
            absent("by", left, wide, (full, block(x, slot)))
        absent("by", left, cov, (slot, full, full, full, full))
    absent("bz", True, blurred, (full, slice(0, LOW), full))
    absent("bz", False, blurred, (full, slice(HIGH, WIDE), full))
    absent("bz", True, cov, (0, 0, 0, full, full))
    absent("bz", False, cov, (0, 0, 2, full, full))
    for rx, ry in ((rx_a, ry_a), (rx_b, ry_b)):
        absent("bx", True, rx, (full, slice(0, 8), full, full))
        absent("bx", False, rx, (full, slice(24, 32), full, full))
        absent("by", True, ry, (full, full, slice(0, 8), full))
        absent("by", False, ry, (full, full, slice(24, 32), full))
    for rz in (rz_a, rz_b):
        absent("bz", True, rz, (full, slice(0, 8), full))
        absent("bz", False, rz, (full, slice(136, 144), full))
    for from_z in (from_za, from_zb):
        absent("bz", True, from_z, (0, full, full, full))
        absent("bz", False, from_z, (1, full, full, full))
    absent("by", True, from_y, (0, full, full, full))
    absent("by", False, from_y, (1, full, full, full))
    absent("bx", True, from_x, (0, full, full))
    absent("bx", False, from_x, (1, full, full))
    rx_a[:, 8:24] = raw[first]
    ry_b[:, :, 8:24] = raw[last]

    kn[...] = jnp.zeros(kn.shape, F32)
    for axis in range(3):
        values = psf_v[:, axis, :]
        kn[axis, 0:VIEWS, 0:TAPS] = values / jnp.sum(values, axis=1, keepdims=True)
    knz[...] = pltpu.roll(kn[2], 1, 1)

    highest = lax.Precision.HIGHEST
    row, lane = iota((XY, XY), 0), iota((XY, XY), 1)
    lane_x, lane_y = lane // SY, lane % SY
    mirror = (row + lane == TAPS - 1).astype(F32)
    kinds = []
    for flip in (False, True):
        for axis, cell, shifts, size in ((0, lane_x, x_shift, SX), (1, lane_y, y_shift, SY)):
            taps = kn[axis]
            if flip:
                taps = jnp.dot(taps, mirror, precision=highest, preferred_element_type=F32)
            taps = pltpu.roll(taps, XY - REACH, 1)
            bands = [
                pltpu.roll(
                    jnp.broadcast_to(taps[view : view + 1, :], (16, XY)), 0, 1, stride=1, stride_axis=0
                )
                for view in range(VIEWS)
            ]
            stack = jnp.concatenate(split(jnp.concatenate(bands, axis=0)), axis=0)
            for shift in shifts:
                place = cell + (-size if flip else size) * shift
                chosen = (row == jnp.where(place < 0, place + XY, place)).astype(BF16)
                both = dot(stack, chosen)
                patterns[len(kinds)] = both[: 16 * VIEWS] + both[16 * VIEWS :]
                kinds.append((flip, axis, shift))
    blur_x, blur_y = 0, xslots
    turn_x, turn_y = xslots + 3, 2 * xslots + 3

    def rows_of(view, i):
        return pl.ds(pl.multiple_of(view * XY + i * 16, 16), 16)

    def pattern(kind, view):
        return patterns[kind, pl.ds(pl.multiple_of(view * 16, 16), 16), :]

    def build_forward(begin, end):
        @pl.loop(begin, end)
        def _(view):
            for x in range(xslots):
                to_x = pattern(turn_x + x, view)
                for y in range(3):
                    to_y = pattern(turn_y + y, view)
                    base = (3 * x + y) * XY
                    for i in range(16):
                        high, low = split(to_y * to_x[i : i + 1, :])
                        kront_h[view, base + i * 16 : base + (i + 1) * 16, :] = high
                        kront_l[view, base + i * 16 : base + (i + 1) * 16, :] = low
            line = jnp.broadcast_to(knz[pl.ds(view, 1), :], (SZ, ROWS))
            band = pltpu.roll(line, 0, 1, stride=1, stride_axis=0)
            fz[view, 0:SZ], fz[view, SZ : 2 * SZ] = split(band)
            bz[view, 0:WIDE], bz[view, WIDE : 2 * WIDE] = split(band.T[0:WIDE])

    def build_adjoint():
        @pl.loop(0, VIEWS)
        def _(view):
            for x in range(xslots):
                to_x = pattern(blur_x + x, view)
                for y in range(3):
                    to_y = pattern(blur_y + y, view)
                    for i in range(16):
                        high, low = split(to_y * to_x[i : i + 1, :])
                        kron_h[rows_of(view, i), block(x, y)] = high
                        kron_l[rows_of(view, i), block(x, y)] = low

    def forward(x, begin, end):
        cut = slice((3 * x + begin) * XY, (3 * x + end) * XY)
        wide_s[0:SZ, cut], wide_s[SZ : 2 * SZ, cut] = split(wide[:, cut])

        @pl.loop(0, VIEWS, step=2)
        def _(pair):
            for view in (pair, pair + 1):
                part = dot3(wide_s[:, cut], kront_h[view, cut, :], kront_l[view, cut, :])
                if x == 0 and begin == 0:
                    blurred[view, LOW:HIGH] = part
                else:
                    blurred[view, LOW:HIGH] = blurred[view, LOW:HIGH] + part

    def turned_y(ry, view, offset):
        return pltpu.roll(ry[view], lax.rem(32 - OFF - offset, 32), 1)[:, 0:SY, :]

    def turned_z(rz, index, offset):
        return pltpu.roll(rz[index], lax.rem(SZ + 16 - OFF - offset, SZ + 16), 0)[0:SZ, :]

    build_forward(0, 2)
    arrive(est_x)
    for x in range(1, xslots):
        start(est_y[x])
    arrive(cov_z)
    start(cov_x)
    arrive(raw_ax)

    @pl.loop(0, half)
    def _(view):
        shifted = rx_a[view, pl.ds(OFF + offsets[0, view], SX), :, :]
        rz_a[view, 8:136, :] = shifted.reshape(XY, SZ).T

    start(raw_az)
    arrive(raw_by)

    @pl.loop(0, half)
    def _(view):
        rx_b[view, 8:24] = turned_y(ry_b, view, offsets[1, half + view])

    start(raw_bx)
    build_forward(2, 4)
    arrive(raw_az)

    @pl.loop(0, half)
    def _(view):
        shifted = turned_z(rz_a, view, offsets[2, view]).T
        ry_a[view, :, 8:24, :] = shifted.reshape(SX, SY, SZ)

    start(raw_ay)
    arrive(cov_x)
    start(cov_y)
    build_forward(4, VIEWS)
    for x in range(xslots):
        forward(x, 0, 1)
    arrive(est_y[0])
    forward(0, 1, 3)
    arrive(raw_bx)

    @pl.loop(0, half)
    def _(view):
        shifted = rx_b[view, pl.ds(OFF + offsets[0, half + view], SX), :, :]
        rz_b[view, 8:136, :] = shifted.reshape(XY, SZ).T

    start(raw_bz)
    for x in range(1, xslots):
        arrive(est_y[x])
        forward(x, 1, 3)
    start(mid_z)
    build_adjoint()

    rest = jnp.zeros((ROWS - WIDE, XY), BF16)

    def ratios(index, base, observed, parts):
        view = base + index
        mask = coverage[0, view].astype(F32)
        high, low = split(blurred[view])
        high = jnp.concatenate([high, rest], axis=0)
        low = jnp.concatenate([low, rest], axis=0)
        high, low = split(mask * observed / dot3(fz[view], high, low))
        parts[index] = dot3(bz[view], high, low)

    back_za, back_zb = [
        [
            to_left("bz", parts.at[:, 0:LOW], from_z.at[1]),
            to_right("bz", parts.at[:, HIGH:WIDE], from_z.at[0]),
        ]
        for parts, from_z in ((part_a, from_za), (part_b, from_zb))
    ]

    def join(index, base, parts, from_z):
        low = parts[index, LOW : LOW + 16] + from_z[0, index]
        high = parts[index, HIGH - 16 : HIGH] + from_z[1, index]
        value = jnp.concatenate([low, parts[index, LOW + 16 : HIGH - 16], high], axis=0)
        columns = slice((base + index) * XY, (base + index + 1) * XY)
        back[0:SZ, columns], back[SZ : 2 * SZ, columns] = split(value)

    arrive(mid_z)
    arrive(raw_bz)
    for index in range(half):
        ratios(index, half, turned_z(rz_b, index, offsets[2, half + index]), part_b)
    start(back_zb)
    arrive(raw_ay)
    for index in range(half):
        shifted = turned_y(ry_a, index, offsets[1, index])
        ratios(index, 0, shifted.reshape(XY, SZ).T, part_a)
    start(back_za)
    arrive(back_zb)
    for index in range(half):
        join(index, half, part_b, from_zb)
    arrive(back_za)
    for index in range(half):
        join(index, 0, part_a, from_za)

    back_y = [
        [
            to_left("by", spread.at[:, block(x, 1)], from_y.at[1, x]),
            to_right("by", spread.at[:, block(x, 2)], from_y.at[0, x]),
        ]
        for x in range(xslots)
    ]
    back_x = [
        to_left("bx", spread.at[:, block(x_left_slot, 0)], from_x.at[1]),
        to_right("bx", spread.at[:, block(x_right_slot, 0)], from_x.at[0]),
    ]
    def add_y(x):
        arrive(back_y[x])
        spread[:, block(x, 0)] = spread[:, block(x, 0)] + (from_y[0, x] + from_y[1, x])

    for x in reversed(range(xslots)):
        for y in (1, 2, 0):
            spread[:, block(x, y)] = dot3(back[...], kron_h[:, block(x, y)], kron_l[:, block(x, y)])
            if y > 0:
                start(back_y[x][y - 1 : y])
    for x in range(1, xslots):
        add_y(x)
    start(back_x)

    arrive(cov_y)

    def factor(axis, position, shift, size):
        cell = position + REACH - row[:, : position.shape[1]] - shift * size
        inside = ((cell >= 0) & (cell < size)).astype(F32)
        return jnp.dot(kn[axis], inside, precision=highest, preferred_element_type=F32)

    factor_x = [factor(0, lane_x, d, SX) for d in x_shift]
    factor_y = [factor(1, lane_y, d, SY) for d in y_shift]
    factor_z = [factor(2, lane[:, :SZ], d, SZ) for d in (-1, 0, 1)]
    rows = []
    for z in range(3):
        total = jnp.zeros((8, XY), F32)
        for y in range(3):
            part = jnp.zeros((8, XY), F32)
            for x in range(xslots):
                part = part + jnp.concatenate([cov[y, x, z]] * 2, axis=1) * factor_x[x]
            total = total + part * factor_y[y]
        rows.append(total)
    weights[...] = jnp.dot(
        jnp.concatenate(factor_z, axis=0).T, jnp.concatenate(rows, axis=0),
        precision=highest, preferred_element_type=F32,
    )

    add_y(0)
    arrive(back_x)
    spread[:, block(0, 0)] = spread[:, block(0, 0)] + (from_x[0] + from_x[1])
    restored = wide[:, block(0, 0)] * spread[:, block(0, 0)] / weights[...]
    out[...] = restored.T.reshape(SX, SY, SZ)
    for copies in [est_x, *est_y, cov_x, cov_y, cov_z, mid_z, raw_ax, raw_ay, raw_bx, raw_by, raw_az, raw_bz]:
        sent(copies)
    for copies in [*back_y, back_x, back_za, back_zb]:
        sent(copies)


def on_device(counts, estimate, raw_views, psf, offsets, coverage):
    xslots = 2 if counts[0] == 2 else 3
    group = 3 * XY
    lanes = xslots * group
    vmem = pl.BlockSpec(memory_space=pltpu.VMEM)
    smem = pl.BlockSpec(memory_space=pltpu.SMEM)
    return pl.pallas_call(
        functools.partial(kernel, counts),
        out_shape=jax.ShapeDtypeStruct(estimate.shape, F32),
        in_specs=[vmem, vmem, vmem, smem, smem],
        out_specs=vmem,
        scratch_shapes=[
            pltpu.VMEM((SZ, lanes), F32),
            pltpu.VMEM((2 * SZ, lanes), BF16),
            pltpu.VMEM((3, xslots, 3, 8, SZ), F32),
            pltpu.VMEM((VIEWS // 2, 32, SY, SZ), F32),
            pltpu.VMEM((VIEWS // 2, 32, SY, SZ), F32),
            pltpu.VMEM((VIEWS // 2, SX, 32, SZ), F32),
            pltpu.VMEM((VIEWS // 2, SX, 32, SZ), F32),
            pltpu.VMEM((VIEWS // 2, SZ + 16, XY), F32),
            pltpu.VMEM((VIEWS // 2, SZ + 16, XY), F32),
            pltpu.VMEM((3, 8, XY), F32),
            pltpu.VMEM((8, XY), F32),
            pltpu.VMEM((2 * xslots + 6, 16 * VIEWS, XY), F32),
            pltpu.VMEM((VIEWS * XY, lanes), BF16),
            pltpu.VMEM((VIEWS * XY, lanes), BF16),
            pltpu.VMEM((VIEWS, lanes, XY), BF16),
            pltpu.VMEM((VIEWS, lanes, XY), BF16),
            pltpu.VMEM((VIEWS, 2 * SZ, ROWS), BF16),
            pltpu.VMEM((VIEWS, 2 * WIDE, SZ), BF16),
            pltpu.VMEM((VIEWS, WIDE, XY), F32),
            pltpu.VMEM((VIEWS // 2, WIDE, XY), F32),
            pltpu.VMEM((VIEWS // 2, WIDE, XY), F32),
            pltpu.VMEM((2 * SZ, VIEWS * XY), BF16),
            pltpu.VMEM((SZ, lanes), F32),
            pltpu.VMEM((2, SZ, XY), F32),
            pltpu.VMEM((2, xslots, SZ, XY), F32),
            pltpu.VMEM((2, VIEWS // 2, 16, XY), F32),
            pltpu.VMEM((2, VIEWS // 2, 16, XY), F32),
            pltpu.VMEM((SZ, XY), F32),
            pltpu.SemaphoreType.DMA((SEMAPHORES,)),
            pltpu.SemaphoreType.DMA((SEMAPHORES,)),
        ],
        compiler_params=pltpu.CompilerParams(
            collective_id=0, has_side_effects=True, vmem_limit_bytes=56 * 1024 * 1024
        ),
    )(
        estimate, raw_views, psf, offsets.T,
        coverage.transpose(1, 2, 3, 0).reshape(1, VIEWS),
    )


def solution(mesh):
    counts = (mesh.shape["bx"], mesh.shape["by"], mesh.shape["bz"])
    return jax.shard_map(
        functools.partial(on_device, counts),
        mesh=mesh,
        in_specs=(
            P("bx", "by", "bz"),
            P(None, "bx", "by", "bz"),
            P(),
            P(),
            P(None, "bx", "by", "bz"),
        ),
        out_specs=P("bx", "by", "bz"),
        check_vma=False,
    )
```

```python
import functools

import jax
import jax.numpy as jnp
from jax import lax
from jax.experimental import pallas as pl
from jax.experimental.pallas import tpu as pltpu
from jax.sharding import PartitionSpec as P

F32 = jnp.float32
BF16 = jnp.bfloat16
MESH = pl.DeviceIdType.MESH
OFF = 8
TAPS = 31
REACH = 15
VIEWS = 6
SEMAPHORES = 48
SX = 16
SY = 16
SZ = 128
XY = SX * SY
LOW, HIGH, WIDE, ROWS = 16, SZ + 16, SZ + 32, 256


def split(value):
    high = value.astype(BF16)
    return high, (value - high.astype(F32)).astype(BF16)


def dot(a, b):
    return jnp.dot(a, b, preferred_element_type=F32)


def iota(shape, dim):
    return lax.broadcasted_iota(jnp.int32, shape, dim)


def dot3(stack, b_high, b_low):
    half = stack.shape[0] // 2
    both = dot(stack, b_high)
    return both[:half] + (both[half:] + dot(stack[:half], b_low))


def kernel(
    counts, est, raw, psf_v, offsets, coverage, out,
    wide, wide_s, cov, rx_a, rx_b, ry_a, ry_b, rz_a, rz_b, kn, knz, patterns,
    kron_h, kron_l, fz, bz,
    blurred, part_a, part_b, back, spread, from_x, from_y, from_za, from_zb, weights, send, recv,
):
    nx, ny, nz = counts
    xslots = 2 if nx == 2 else 3
    group = 3 * XY
    lanes = xslots * group
    ix, iy, iz = lax.axis_index("bx"), lax.axis_index("by"), lax.axis_index("bz")
    where = {"bx": (ix, nx), "by": (iy, ny), "bz": (iz, nz)}
    has_left = {name: i > 0 for name, (i, n) in where.items()}
    has_right = {name: i < n - 1 for name, (i, n) in where.items()}
    x_shift = [0, 1 - 2 * ix] if nx == 2 else [0, -1, 1]
    y_shift = [0, -1, 1]
    x_left_slot = 1
    x_right_slot = 1 if nx == 2 else 2
    used = iter(range(SEMAPHORES))

    def to_side(axis, left, src, dst):
        index = next(used)
        return axis, left, pltpu.make_async_remote_copy(
            src_ref=src, dst_ref=dst, send_sem=send.at[index], recv_sem=recv.at[index],
            device_id={axis: where[axis][0] + (-1 if left else 1)}, device_id_type=MESH,
        )

    def to_left(axis, src, dst):
        return to_side(axis, True, src, dst)

    def to_right(axis, src, dst):
        return to_side(axis, False, src, dst)

    def start(copies):
        for axis, left, copy in copies:
            @pl.when(has_left[axis] if left else has_right[axis])
            def _():
                copy.start()

    def arrive(copies):
        for axis, left, copy in copies:
            @pl.when(has_right[axis] if left else has_left[axis])
            def _():
                copy.wait_recv()

    def sent(copies):
        for axis, left, copy in copies:
            @pl.when(has_left[axis] if left else has_right[axis])
            def _():
                copy.wait_send()

    def absent(axis, left, ref, index):
        @pl.when(jnp.logical_not(has_left[axis] if left else has_right[axis]))
        def _():
            ref[index] = jnp.zeros(ref.at[index].shape, ref.dtype)

    def block(x, y):
        return slice((3 * x + y) * XY, (3 * x + y + 1) * XY)

    full = slice(None)

    barrier = pltpu.get_barrier_semaphore()
    for axis, (i, n) in where.items():
        @pl.when(has_left[axis])
        def _():
            pl.semaphore_signal(barrier, inc=1, device_id={axis: i - 1}, device_id_type=MESH)

        @pl.when(has_right[axis])
        def _():
            pl.semaphore_signal(barrier, inc=1, device_id={axis: i + 1}, device_id_type=MESH)

    wide[:, block(0, 0)] = est[...].reshape(XY, SZ).T
    cov_rows = jnp.zeros((8, SZ), F32)
    for view in range(VIEWS):
        value = coverage[0, view].astype(F32)
        cov_rows = jnp.where(iota((8, SZ), 0) == view, value, cov_rows)
    cov[0, 0, 1] = cov_rows

    degree = sum(
        (has_left[axis].astype(jnp.int32) + has_right[axis].astype(jnp.int32) for axis in where),
        jnp.int32(0),
    )
    pl.semaphore_wait(barrier, degree)

    half = VIEWS // 2
    first, last = slice(0, half), slice(half, VIEWS)
    est_x = [
        to_left("bx", wide.at[:, block(0, 0)], wide.at[:, block(x_right_slot, 0)]),
        to_right("bx", wide.at[:, block(0, 0)], wide.at[:, block(x_left_slot, 0)]),
    ]
    cov_z = [
        to_left("bz", cov.at[0, 0, 1], cov.at[0, 0, 2]),
        to_right("bz", cov.at[0, 0, 1], cov.at[0, 0, 0]),
    ]
    cov_x = [
        to_left("bx", cov.at[0, 0], cov.at[0, x_right_slot]),
        to_right("bx", cov.at[0, 0], cov.at[0, x_left_slot]),
    ]
    est_y = [
        [
            to_left("by", wide.at[:, block(x, 0)], wide.at[:, block(x, 2)]),
            to_right("by", wide.at[:, block(x, 0)], wide.at[:, block(x, 1)]),
        ]
        for x in range(xslots)
    ]
    cov_y = [
        to_left("by", cov.at[0], cov.at[2]),
        to_right("by", cov.at[0], cov.at[1]),
    ]
    raw_ax = [
        to_left("bx", raw.at[first, 0:8], rx_a.at[:, 24:32]),
        to_right("bx", raw.at[first, 8:16], rx_a.at[:, 0:8]),
    ]
    raw_ay = [
        to_left("by", ry_a.at[:, :, 8:16], ry_a.at[:, :, 24:32]),
        to_right("by", ry_a.at[:, :, 16:24], ry_a.at[:, :, 0:8]),
    ]
    raw_by = [
        to_left("by", raw.at[last, :, 0:8], ry_b.at[:, :, 24:32]),
        to_right("by", raw.at[last, :, 8:16], ry_b.at[:, :, 0:8]),
    ]
    raw_bx = [
        to_left("bx", rx_b.at[:, 8:16], rx_b.at[:, 24:32]),
        to_right("bx", rx_b.at[:, 16:24], rx_b.at[:, 0:8]),
    ]
    raw_az, raw_bz = [
        [
            to_left("bz", rz.at[:, 8:16], rz.at[:, 136:144]),
            to_right("bz", rz.at[:, 128:136], rz.at[:, 0:8]),
        ]
        for rz in (rz_a, rz_b)
    ]

    mid_z = [
        to_left("bz", blurred.at[:, LOW : LOW + 16], blurred.at[:, HIGH:WIDE]),
        to_right("bz", blurred.at[:, HIGH - 16 : HIGH], blurred.at[:, 0:LOW]),
    ]

    start(est_x)
    start(est_y[0])
    start(cov_z)
    start(raw_by)
    start(raw_ax)

    if nx > 2:
        for left, slot in ((True, x_left_slot), (False, x_right_slot)):
            absent("bx", left, wide, (full, block(slot, 0)))
            absent("bx", left, cov, (0, slot, full, full, full))
    for left, slot in ((True, 1), (False, 2)):
        for x in range(xslots):
            absent("by", left, wide, (full, block(x, slot)))
        absent("by", left, cov, (slot, full, full, full, full))
    absent("bz", True, blurred, (full, slice(0, LOW), full))
    absent("bz", False, blurred, (full, slice(HIGH, WIDE), full))
    absent("bz", True, cov, (0, 0, 0, full, full))
    absent("bz", False, cov, (0, 0, 2, full, full))
    for rx, ry in ((rx_a, ry_a), (rx_b, ry_b)):
        absent("bx", True, rx, (full, slice(0, 8), full, full))
        absent("bx", False, rx, (full, slice(24, 32), full, full))
        absent("by", True, ry, (full, full, slice(0, 8), full))
        absent("by", False, ry, (full, full, slice(24, 32), full))
    for rz in (rz_a, rz_b):
        absent("bz", True, rz, (full, slice(0, 8), full))
        absent("bz", False, rz, (full, slice(136, 144), full))
    for from_z in (from_za, from_zb):
        absent("bz", True, from_z, (0, full, full, full))
        absent("bz", False, from_z, (1, full, full, full))
    absent("by", True, from_y, (0, full, full, full))
    absent("by", False, from_y, (1, full, full, full))
    absent("bx", True, from_x, (0, full, full))
    absent("bx", False, from_x, (1, full, full))
    rx_a[:, 8:24] = raw[first]
    ry_b[:, :, 8:24] = raw[last]

    kn[...] = jnp.zeros(kn.shape, F32)
    for axis in range(3):
        values = psf_v[:, axis, :]
        kn[axis, 0:VIEWS, 0:TAPS] = values / jnp.sum(values, axis=1, keepdims=True)
    knz[...] = pltpu.roll(kn[2], 1, 1)

    highest = lax.Precision.HIGHEST
    row, lane = iota((XY, XY), 0), iota((XY, XY), 1)
    lane_x, lane_y = lane // SY, lane % SY
    mirror = (row + lane == TAPS - 1).astype(F32)
    kind = 0
    for axis, cell, shifts, size in ((0, lane_x, x_shift, SX), (1, lane_y, y_shift, SY)):
        taps = jnp.dot(kn[axis], mirror, precision=highest, preferred_element_type=F32)
        taps = pltpu.roll(taps, XY - REACH, 1)
        bands = [
            pltpu.roll(
                jnp.broadcast_to(taps[view : view + 1, :], (16, XY)), 0, 1, stride=1, stride_axis=0
            )
            for view in range(VIEWS)
        ]
        stack = jnp.concatenate(split(jnp.concatenate(bands, axis=0)), axis=0)
        for shift in shifts:
            place = cell - size * shift
            chosen = (row == jnp.where(place < 0, place + XY, place)).astype(BF16)
            both = dot(stack, chosen)
            patterns[kind] = both[: 16 * VIEWS] + both[16 * VIEWS :]
            kind += 1

    def columns_of(view):
        return pl.ds(pl.multiple_of(view * XY, XY), XY)

    def pattern(kind, view):
        return patterns[kind, pl.ds(pl.multiple_of(view * 16, 16), 16), :]

    def build_forward(begin, end):
        @pl.loop(begin, end)
        def _(view):
            for x in range(xslots):
                to_x = pattern(x, view)
                for y in range(3):
                    to_y = pattern(xslots + y, view)
                    base = (3 * x + y) * XY
                    for i in range(16):
                        high, low = split(to_y * to_x[i : i + 1, :])
                        kron_h[base + i * 16 : base + (i + 1) * 16, columns_of(view)] = high
                        kron_l[base + i * 16 : base + (i + 1) * 16, columns_of(view)] = low
            line = jnp.broadcast_to(knz[pl.ds(view, 1), :], (SZ, ROWS))
            band = pltpu.roll(line, 0, 1, stride=1, stride_axis=0)
            fz[view, 0:SZ], fz[view, SZ : 2 * SZ] = split(band)
            bz[view, 0:WIDE], bz[view, WIDE : 2 * WIDE] = split(band.T[0:WIDE])

    def forward(x, begin, end):
        cut = slice((3 * x + begin) * XY, (3 * x + end) * XY)
        wide_s[0:SZ, cut], wide_s[SZ : 2 * SZ, cut] = split(wide[:, cut])

        @pl.loop(0, VIEWS, step=2)
        def _(pair):
            for view in (pair, pair + 1):
                columns = columns_of(view)
                part = dot3(wide_s[:, cut], kron_h[cut, columns], kron_l[cut, columns])
                if x == 0 and begin == 0:
                    blurred[view, LOW:HIGH] = part
                else:
                    blurred[view, LOW:HIGH] = blurred[view, LOW:HIGH] + part

    def turned_y(ry, view, offset):
        return pltpu.roll(ry[view], lax.rem(32 - OFF - offset, 32), 1)[:, 0:SY, :]

    def turned_z(rz, index, offset):
        return pltpu.roll(rz[index], lax.rem(SZ + 16 - OFF - offset, SZ + 16), 0)[0:SZ, :]

    build_forward(0, 2)
    arrive(est_x)
    for x in range(1, xslots):
        start(est_y[x])
    arrive(cov_z)
    start(cov_x)
    arrive(raw_ax)

    @pl.loop(0, half)
    def _(view):
        shifted = rx_a[view, pl.ds(OFF + offsets[0, view], SX), :, :]
        rz_a[view, 8:136, :] = shifted.reshape(XY, SZ).T

    start(raw_az)
    arrive(raw_by)

    @pl.loop(0, half)
    def _(view):
        rx_b[view, 8:24] = turned_y(ry_b, view, offsets[1, half + view])

    start(raw_bx)
    build_forward(2, 4)
    arrive(raw_az)

    @pl.loop(0, half)
    def _(view):
        shifted = turned_z(rz_a, view, offsets[2, view]).T
        ry_a[view, :, 8:24, :] = shifted.reshape(SX, SY, SZ)

    start(raw_ay)
    arrive(cov_x)
    start(cov_y)
    build_forward(4, VIEWS)
    for x in range(xslots):
        forward(x, 0, 1)
    arrive(est_y[0])
    forward(0, 1, 3)
    arrive(raw_bx)

    @pl.loop(0, half)
    def _(view):
        shifted = rx_b[view, pl.ds(OFF + offsets[0, half + view], SX), :, :]
        rz_b[view, 8:136, :] = shifted.reshape(XY, SZ).T

    start(raw_bz)
    for x in range(1, xslots):
        arrive(est_y[x])
        forward(x, 1, 3)
    start(mid_z)

    rest = jnp.zeros((ROWS - WIDE, XY), BF16)

    def ratios(index, base, observed, parts):
        view = base + index
        mask = coverage[0, view].astype(F32)
        high, low = split(blurred[view])
        high = jnp.concatenate([high, rest], axis=0)
        low = jnp.concatenate([low, rest], axis=0)
        high, low = split(mask * observed / dot3(fz[view], high, low))
        parts[index] = dot3(bz[view], high, low)

    back_za, back_zb = [
        [
            to_left("bz", parts.at[:, 0:LOW], from_z.at[1]),
            to_right("bz", parts.at[:, HIGH:WIDE], from_z.at[0]),
        ]
        for parts, from_z in ((part_a, from_za), (part_b, from_zb))
    ]

    def join(index, base, parts, from_z):
        low = parts[index, LOW : LOW + 16] + from_z[0, index]
        high = parts[index, HIGH - 16 : HIGH] + from_z[1, index]
        value = jnp.concatenate([low, parts[index, LOW + 16 : HIGH - 16], high], axis=0)
        rows_of = slice((base + index) * XY, (base + index + 1) * XY)
        back[rows_of, 0:SZ], back[rows_of, SZ : 2 * SZ] = split(value.T)

    arrive(mid_z)
    arrive(raw_bz)
    for index in range(half):
        ratios(index, half, turned_z(rz_b, index, offsets[2, half + index]), part_b)
    start(back_zb)
    arrive(raw_ay)
    for index in range(half):
        shifted = turned_y(ry_a, index, offsets[1, index])
        ratios(index, 0, shifted.reshape(XY, SZ).T, part_a)
    start(back_za)
    arrive(back_zb)
    for index in range(half):
        join(index, half, part_b, from_zb)
    arrive(back_za)
    for index in range(half):
        join(index, 0, part_a, from_za)

    back_y = [
        [
            to_left("by", spread.at[block(x, 1)], from_y.at[1, x]),
            to_right("by", spread.at[block(x, 2)], from_y.at[0, x]),
        ]
        for x in range(xslots)
    ]
    back_x = [
        to_left("bx", spread.at[block(x_left_slot, 0)], from_x.at[1]),
        to_right("bx", spread.at[block(x_right_slot, 0)], from_x.at[0]),
    ]
    def add_y(x):
        arrive(back_y[x])
        spread[block(x, 0)] = spread[block(x, 0)] + (from_y[0, x] + from_y[1, x])

    for x in reversed(range(xslots)):
        for y in (1, 2, 0):
            both = dot(kron_h[block(x, y), :], back[...])
            low = dot(kron_l[block(x, y), :], back[:, 0:SZ])
            spread[block(x, y)] = both[:, 0:SZ] + (both[:, SZ : 2 * SZ] + low)
            if y > 0:
                start(back_y[x][y - 1 : y])
    for x in range(1, xslots):
        add_y(x)
    start(back_x)

    arrive(cov_y)

    def factor(axis, position, shift, size):
        cell = position + REACH - row[:, : position.shape[1]] - shift * size
        inside = ((cell >= 0) & (cell < size)).astype(F32)
        return jnp.dot(kn[axis], inside, precision=highest, preferred_element_type=F32)

    factor_x = [factor(0, lane_x, d, SX) for d in x_shift]
    factor_y = [factor(1, lane_y, d, SY) for d in y_shift]
    factor_z = [factor(2, lane[:, :SZ], d, SZ) for d in (-1, 0, 1)]
    rows = []
    for z in range(3):
        total = jnp.zeros((8, XY), F32)
        for y in range(3):
            part = jnp.zeros((8, XY), F32)
            for x in range(xslots):
                part = part + jnp.concatenate([cov[y, x, z]] * 2, axis=1) * factor_x[x]
            total = total + part * factor_y[y]
        rows.append(total)
    weights[...] = jnp.dot(
        jnp.concatenate(rows, axis=0).T, jnp.concatenate(factor_z, axis=0),
        precision=highest, preferred_element_type=F32,
    )

    add_y(0)
    arrive(back_x)
    total = spread[block(0, 0)] + (from_x[0] + from_x[1])
    restored = est[...].reshape(XY, SZ) * total / weights[...]
    out[...] = restored.reshape(SX, SY, SZ)
    for copies in [est_x, *est_y, cov_x, cov_y, cov_z, mid_z, raw_ax, raw_ay, raw_bx, raw_by, raw_az, raw_bz]:
        sent(copies)
    for copies in [*back_y, back_x, back_za, back_zb]:
        sent(copies)


def on_device(counts, estimate, raw_views, psf, offsets, coverage):
    xslots = 2 if counts[0] == 2 else 3
    group = 3 * XY
    lanes = xslots * group
    vmem = pl.BlockSpec(memory_space=pltpu.VMEM)
    smem = pl.BlockSpec(memory_space=pltpu.SMEM)
    return pl.pallas_call(
        functools.partial(kernel, counts),
        out_shape=jax.ShapeDtypeStruct(estimate.shape, F32),
        in_specs=[vmem, vmem, vmem, smem, smem],
        out_specs=vmem,
        scratch_shapes=[
            pltpu.VMEM((SZ, lanes), F32),
            pltpu.VMEM((2 * SZ, lanes), BF16),
            pltpu.VMEM((3, xslots, 3, 8, SZ), F32),
            pltpu.VMEM((VIEWS // 2, 32, SY, SZ), F32),
            pltpu.VMEM((VIEWS // 2, 32, SY, SZ), F32),
            pltpu.VMEM((VIEWS // 2, SX, 32, SZ), F32),
            pltpu.VMEM((VIEWS // 2, SX, 32, SZ), F32),
            pltpu.VMEM((VIEWS // 2, SZ + 16, XY), F32),
            pltpu.VMEM((VIEWS // 2, SZ + 16, XY), F32),
            pltpu.VMEM((3, 8, XY), F32),
            pltpu.VMEM((8, XY), F32),
            pltpu.VMEM((xslots + 3, 16 * VIEWS, XY), F32),
            pltpu.VMEM((lanes, VIEWS * XY), BF16),
            pltpu.VMEM((lanes, VIEWS * XY), BF16),
            pltpu.VMEM((VIEWS, 2 * SZ, ROWS), BF16),
            pltpu.VMEM((VIEWS, 2 * WIDE, SZ), BF16),
            pltpu.VMEM((VIEWS, WIDE, XY), F32),
            pltpu.VMEM((VIEWS // 2, WIDE, XY), F32),
            pltpu.VMEM((VIEWS // 2, WIDE, XY), F32),
            pltpu.VMEM((VIEWS * XY, 2 * SZ), BF16),
            pltpu.VMEM((lanes, SZ), F32),
            pltpu.VMEM((2, XY, SZ), F32),
            pltpu.VMEM((2, xslots, XY, SZ), F32),
            pltpu.VMEM((2, VIEWS // 2, 16, XY), F32),
            pltpu.VMEM((2, VIEWS // 2, 16, XY), F32),
            pltpu.VMEM((XY, SZ), F32),
            pltpu.SemaphoreType.DMA((SEMAPHORES,)),
            pltpu.SemaphoreType.DMA((SEMAPHORES,)),
        ],
        compiler_params=pltpu.CompilerParams(
            collective_id=0, has_side_effects=True, vmem_limit_bytes=56 * 1024 * 1024
        ),
    )(
        estimate, raw_views, psf, offsets.T,
        coverage.transpose(1, 2, 3, 0).reshape(1, VIEWS),
    )


def solution(mesh):
    counts = (mesh.shape["bx"], mesh.shape["by"], mesh.shape["bz"])
    return jax.shard_map(
        functools.partial(on_device, counts),
        mesh=mesh,
        in_specs=(
            P("bx", "by", "bz"),
            P(None, "bx", "by", "bz"),
            P(),
            P(),
            P(None, "bx", "by", "bz"),
        ),
        out_specs=P("bx", "by", "bz"),
        check_vma=False,
    )
```

```python
import functools

import jax
import jax.numpy as jnp
from jax import lax
from jax.experimental import pallas as pl
from jax.experimental.pallas import tpu as pltpu
from jax.sharding import PartitionSpec as P

F32 = jnp.float32
BF16 = jnp.bfloat16
MESH = pl.DeviceIdType.MESH
OFF = 8
TAPS = 31
REACH = 15
VIEWS = 6
SEMAPHORES = 48
SX = 16
SY = 16
SZ = 128
XY = SX * SY
LOW, HIGH, WIDE, ROWS = 16, SZ + 16, SZ + 32, 256


def split(value):
    high = value.astype(BF16)
    return high, (value - high.astype(F32)).astype(BF16)


def dot(a, b):
    return jnp.dot(a, b, preferred_element_type=F32)


def iota(shape, dim):
    return lax.broadcasted_iota(jnp.int32, shape, dim)


def dot3(stack, b_high, b_low):
    half = stack.shape[0] // 2
    both = dot(stack, b_high)
    return both[:half] + (both[half:] + dot(stack[:half], b_low))


def kernel(
    counts, est, raw, psf_v, offsets, coverage, out,
    wide, wide_s, cov, rx_a, rx_b, ry_a, ry_b, rz_a, rz_b, kn, knz, patterns,
    kron_h, kron_l, fz, bz,
    blurred, part_a, part_b, back, spread, from_x, from_y, from_za, from_zb, weights, send, recv, local,
):
    nx, ny, nz = counts
    xslots = 2 if nx == 2 else 3
    group = 3 * XY
    lanes = xslots * group
    ix, iy, iz = lax.axis_index("bx"), lax.axis_index("by"), lax.axis_index("bz")
    where = {"bx": (ix, nx), "by": (iy, ny), "bz": (iz, nz)}
    has_left = {name: i > 0 for name, (i, n) in where.items()}
    has_right = {name: i < n - 1 for name, (i, n) in where.items()}
    x_shift = [0, 1 - 2 * ix] if nx == 2 else [0, -1, 1]
    y_shift = [0, -1, 1]
    x_left_slot = 1
    x_right_slot = 1 if nx == 2 else 2
    used = iter(range(SEMAPHORES))

    def to_side(axis, left, src, dst):
        index = next(used)
        return axis, left, pltpu.make_async_remote_copy(
            src_ref=src, dst_ref=dst, send_sem=send.at[index], recv_sem=recv.at[index],
            device_id={axis: where[axis][0] + (-1 if left else 1)}, device_id_type=MESH,
        )

    def to_left(axis, src, dst):
        return to_side(axis, True, src, dst)

    def to_right(axis, src, dst):
        return to_side(axis, False, src, dst)

    def start(copies):
        for axis, left, copy in copies:
            @pl.when(has_left[axis] if left else has_right[axis])
            def _():
                copy.start()

    def arrive(copies):
        for axis, left, copy in copies:
            @pl.when(has_right[axis] if left else has_left[axis])
            def _():
                copy.wait_recv()

    def sent(copies):
        for axis, left, copy in copies:
            @pl.when(has_left[axis] if left else has_right[axis])
            def _():
                copy.wait_send()

    def absent(axis, left, ref, index):
        @pl.when(jnp.logical_not(has_left[axis] if left else has_right[axis]))
        def _():
            ref[index] = jnp.zeros(ref.at[index].shape, ref.dtype)

    def block(x, y):
        return slice((3 * x + y) * XY, (3 * x + y + 1) * XY)

    full = slice(None)

    barrier = pltpu.get_barrier_semaphore()
    for axis, (i, n) in where.items():
        @pl.when(has_left[axis])
        def _():
            pl.semaphore_signal(barrier, inc=1, device_id={axis: i - 1}, device_id_type=MESH)

        @pl.when(has_right[axis])
        def _():
            pl.semaphore_signal(barrier, inc=1, device_id={axis: i + 1}, device_id_type=MESH)

    wide[:, block(0, 0)] = est[...].reshape(XY, SZ).T
    cov_rows = jnp.zeros((8, SZ), F32)
    for view in range(VIEWS):
        value = coverage[0, view].astype(F32)
        cov_rows = jnp.where(iota((8, SZ), 0) == view, value, cov_rows)
    cov[0, 0, 1] = cov_rows

    degree = sum(
        (has_left[axis].astype(jnp.int32) + has_right[axis].astype(jnp.int32) for axis in where),
        jnp.int32(0),
    )
    pl.semaphore_wait(barrier, degree)

    half = VIEWS // 2
    first, last = slice(0, half), slice(half, VIEWS)
    est_x = [
        to_left("bx", wide.at[:, block(0, 0)], wide.at[:, block(x_right_slot, 0)]),
        to_right("bx", wide.at[:, block(0, 0)], wide.at[:, block(x_left_slot, 0)]),
    ]
    cov_z = [
        to_left("bz", cov.at[0, 0, 1], cov.at[0, 0, 2]),
        to_right("bz", cov.at[0, 0, 1], cov.at[0, 0, 0]),
    ]
    cov_x = [
        to_left("bx", cov.at[0, 0], cov.at[0, x_right_slot]),
        to_right("bx", cov.at[0, 0], cov.at[0, x_left_slot]),
    ]
    est_y = [
        [
            to_left("by", wide.at[:, block(x, 0)], wide.at[:, block(x, 2)]),
            to_right("by", wide.at[:, block(x, 0)], wide.at[:, block(x, 1)]),
        ]
        for x in range(xslots)
    ]
    cov_y = [
        to_left("by", cov.at[0], cov.at[2]),
        to_right("by", cov.at[0], cov.at[1]),
    ]
    raw_ax = [
        to_left("bx", raw.at[first, 0:8], rx_a.at[:, 24:32]),
        to_right("bx", raw.at[first, 8:16], rx_a.at[:, 0:8]),
    ]
    raw_ay = [
        to_left("by", ry_a.at[:, :, 8:16], ry_a.at[:, :, 24:32]),
        to_right("by", ry_a.at[:, :, 16:24], ry_a.at[:, :, 0:8]),
    ]
    raw_by = [
        to_left("by", raw.at[last, :, 0:8], ry_b.at[:, :, 24:32]),
        to_right("by", raw.at[last, :, 8:16], ry_b.at[:, :, 0:8]),
    ]
    raw_bx = [
        to_left("bx", rx_b.at[:, 8:16], rx_b.at[:, 24:32]),
        to_right("bx", rx_b.at[:, 16:24], rx_b.at[:, 0:8]),
    ]
    raw_az, raw_bz = [
        [
            to_left("bz", rz.at[:, 8:16], rz.at[:, 136:144]),
            to_right("bz", rz.at[:, 128:136], rz.at[:, 0:8]),
        ]
        for rz in (rz_a, rz_b)
    ]

    mid_z = [
        to_left("bz", blurred.at[:, LOW : LOW + 16], blurred.at[:, HIGH:WIDE]),
        to_right("bz", blurred.at[:, HIGH - 16 : HIGH], blurred.at[:, 0:LOW]),
    ]

    start(est_x)
    start(est_y[0])
    start(cov_z)
    start(raw_by)
    start(raw_ax)

    if nx > 2:
        for left, slot in ((True, x_left_slot), (False, x_right_slot)):
            absent("bx", left, wide, (full, block(slot, 0)))
            absent("bx", left, cov, (0, slot, full, full, full))
    for left, slot in ((True, 1), (False, 2)):
        for x in range(xslots):
            absent("by", left, wide, (full, block(x, slot)))
        absent("by", left, cov, (slot, full, full, full, full))
    absent("bz", True, blurred, (full, slice(0, LOW), full))
    absent("bz", False, blurred, (full, slice(HIGH, WIDE), full))
    absent("bz", True, cov, (0, 0, 0, full, full))
    absent("bz", False, cov, (0, 0, 2, full, full))
    for rx, ry in ((rx_a, ry_a), (rx_b, ry_b)):
        absent("bx", True, rx, (full, slice(0, 8), full, full))
        absent("bx", False, rx, (full, slice(24, 32), full, full))
        absent("by", True, ry, (full, full, slice(0, 8), full))
        absent("by", False, ry, (full, full, slice(24, 32), full))
    for rz in (rz_a, rz_b):
        absent("bz", True, rz, (full, slice(0, 8), full))
        absent("bz", False, rz, (full, slice(136, 144), full))
    for from_z in (from_za, from_zb):
        absent("bz", True, from_z, (0, full, full, full))
        absent("bz", False, from_z, (1, full, full, full))
    absent("by", True, from_y, (0, full, full, full))
    absent("by", False, from_y, (1, full, full, full))
    absent("bx", True, from_x, (0, full, full))
    absent("bx", False, from_x, (1, full, full))
    own_a = pltpu.make_async_copy(raw.at[first], rx_a.at[:, 8:24], local.at[0])
    own_b = pltpu.make_async_copy(raw.at[last], ry_b.at[:, :, 8:24], local.at[1])
    own_a.start()
    own_b.start()

    kn[...] = jnp.zeros(kn.shape, F32)
    for axis in range(3):
        values = psf_v[:, axis, :]
        kn[axis, 0:VIEWS, 0:TAPS] = values / jnp.sum(values, axis=1, keepdims=True)
    knz[...] = pltpu.roll(kn[2], 1, 1)

    highest = lax.Precision.HIGHEST
    row, lane = iota((XY, XY), 0), iota((XY, XY), 1)
    lane_x, lane_y = lane // SY, lane % SY
    mirror = (row + lane == TAPS - 1).astype(F32)
    kind = 0
    for axis, cell, shifts, size in ((0, lane_x, x_shift, SX), (1, lane_y, y_shift, SY)):
        taps = jnp.dot(kn[axis], mirror, precision=highest, preferred_element_type=F32)
        taps = pltpu.roll(taps, XY - REACH, 1)
        bands = [
            pltpu.roll(
                jnp.broadcast_to(taps[view : view + 1, :], (16, XY)), 0, 1, stride=1, stride_axis=0
            )
            for view in range(VIEWS)
        ]
        stack = jnp.concatenate(split(jnp.concatenate(bands, axis=0)), axis=0)
        for shift in shifts:
            place = cell - size * shift
            chosen = (row == jnp.where(place < 0, place + XY, place)).astype(BF16)
            both = dot(stack, chosen)
            patterns[kind] = both[: 16 * VIEWS] + both[16 * VIEWS :]
            kind += 1

    def columns_of(view):
        return pl.ds(pl.multiple_of(view * XY, XY), XY)

    def pattern(kind, view):
        return patterns[kind, pl.ds(pl.multiple_of(view * 16, 16), 16), :]

    def build_forward(begin, end):
        @pl.loop(begin, end)
        def _(view):
            for x in range(xslots):
                to_x = pattern(x, view)
                for y in range(3):
                    to_y = pattern(xslots + y, view)
                    base = (3 * x + y) * XY
                    for i in range(16):
                        high, low = split(to_y * to_x[i : i + 1, :])
                        kron_h[base + i * 16 : base + (i + 1) * 16, columns_of(view)] = high
                        kron_l[base + i * 16 : base + (i + 1) * 16, columns_of(view)] = low
            line = jnp.broadcast_to(knz[pl.ds(view, 1), :], (SZ, ROWS))
            band = pltpu.roll(line, 0, 1, stride=1, stride_axis=0)
            fz[view, 0:SZ], fz[view, SZ : 2 * SZ] = split(band)
            bz[view, 0:WIDE], bz[view, WIDE : 2 * WIDE] = split(band.T[0:WIDE])

    def forward(x, begin, end):
        cut = slice((3 * x + begin) * XY, (3 * x + end) * XY)
        wide_s[0:SZ, cut], wide_s[SZ : 2 * SZ, cut] = split(wide[:, cut])

        @pl.loop(0, VIEWS, step=2)
        def _(pair):
            for view in (pair, pair + 1):
                columns = columns_of(view)
                part = dot3(wide_s[:, cut], kron_h[cut, columns], kron_l[cut, columns])
                if x == 0 and begin == 0:
                    blurred[view, LOW:HIGH] = part
                else:
                    blurred[view, LOW:HIGH] = blurred[view, LOW:HIGH] + part

    def turned_y(ry, view, offset):
        return pltpu.roll(ry[view], lax.rem(32 - OFF - offset, 32), 1)[:, 0:SY, :]

    def turned_z(rz, index, offset):
        return pltpu.roll(rz[index], lax.rem(SZ + 16 - OFF - offset, SZ + 16), 0)[0:SZ, :]

    build_forward(0, 2)
    arrive(est_x)
    for x in range(1, xslots):
        start(est_y[x])
    arrive(cov_z)
    start(cov_x)
    own_a.wait()
    arrive(raw_ax)

    @pl.loop(0, half)
    def _(view):
        shifted = rx_a[view, pl.ds(OFF + offsets[0, view], SX), :, :]
        rz_a[view, 8:136, :] = shifted.reshape(XY, SZ).T

    start(raw_az)
    own_b.wait()
    arrive(raw_by)

    @pl.loop(0, half)
    def _(view):
        rx_b[view, 8:24] = turned_y(ry_b, view, offsets[1, half + view])

    start(raw_bx)
    build_forward(2, 4)
    arrive(raw_az)

    @pl.loop(0, half)
    def _(view):
        shifted = turned_z(rz_a, view, offsets[2, view]).T
        ry_a[view, :, 8:24, :] = shifted.reshape(SX, SY, SZ)

    start(raw_ay)
    arrive(cov_x)
    start(cov_y)
    build_forward(4, VIEWS)
    for x in range(xslots):
        forward(x, 0, 1)
    arrive(est_y[0])
    forward(0, 1, 3)
    arrive(raw_bx)

    @pl.loop(0, half)
    def _(view):
        shifted = rx_b[view, pl.ds(OFF + offsets[0, half + view], SX), :, :]
        rz_b[view, 8:136, :] = shifted.reshape(XY, SZ).T

    start(raw_bz)
    for x in range(1, xslots):
        arrive(est_y[x])
        forward(x, 1, 3)
    start(mid_z)

    rest = jnp.zeros((ROWS - WIDE, XY), BF16)

    def ratios(index, base, observed, parts):
        view = base + index
        mask = coverage[0, view].astype(F32)
        high, low = split(blurred[view])
        high = jnp.concatenate([high, rest], axis=0)
        low = jnp.concatenate([low, rest], axis=0)
        high, low = split(mask * observed / dot3(fz[view], high, low))
        parts[index] = dot3(bz[view], high, low)

    back_za, back_zb = [
        [
            to_left("bz", parts.at[:, 0:LOW], from_z.at[1]),
            to_right("bz", parts.at[:, HIGH:WIDE], from_z.at[0]),
        ]
        for parts, from_z in ((part_a, from_za), (part_b, from_zb))
    ]

    def join(index, base, parts, from_z):
        low = parts[index, LOW : LOW + 16] + from_z[0, index]
        high = parts[index, HIGH - 16 : HIGH] + from_z[1, index]
        value = jnp.concatenate([low, parts[index, LOW + 16 : HIGH - 16], high], axis=0)
        rows_of = slice((base + index) * XY, (base + index + 1) * XY)
        back[rows_of, 0:SZ], back[rows_of, SZ : 2 * SZ] = split(value.T)

    arrive(mid_z)
    arrive(raw_bz)
    for index in range(half):
        ratios(index, half, turned_z(rz_b, index, offsets[2, half + index]), part_b)
    start(back_zb)

    arrive(cov_y)

    def factor(axis, position, shift, size):
        cell = position + REACH - row[:, : position.shape[1]] - shift * size
        inside = ((cell >= 0) & (cell < size)).astype(F32)
        return jnp.dot(kn[axis], inside, precision=highest, preferred_element_type=F32)

    factor_x = [factor(0, lane_x, d, SX) for d in x_shift]
    factor_y = [factor(1, lane_y, d, SY) for d in y_shift]
    factor_z = [factor(2, lane[:, :SZ], d, SZ) for d in (-1, 0, 1)]
    rows = []
    for z in range(3):
        total = jnp.zeros((8, XY), F32)
        for y in range(3):
            part = jnp.zeros((8, XY), F32)
            for x in range(xslots):
                part = part + jnp.concatenate([cov[y, x, z]] * 2, axis=1) * factor_x[x]
            total = total + part * factor_y[y]
        rows.append(total)
    weights[...] = jnp.dot(
        jnp.concatenate(rows, axis=0).T, jnp.concatenate(factor_z, axis=0),
        precision=highest, preferred_element_type=F32,
    )

    arrive(raw_ay)
    for index in range(half):
        shifted = turned_y(ry_a, index, offsets[1, index])
        ratios(index, 0, shifted.reshape(XY, SZ).T, part_a)
    start(back_za)
    arrive(back_zb)
    for index in range(half):
        join(index, half, part_b, from_zb)
    arrive(back_za)
    for index in range(half):
        join(index, 0, part_a, from_za)

    back_y = [
        [
            to_left("by", spread.at[block(x, 1)], from_y.at[1, x]),
            to_right("by", spread.at[block(x, 2)], from_y.at[0, x]),
        ]
        for x in range(xslots)
    ]
    back_x = [
        to_left("bx", spread.at[block(x_left_slot, 0)], from_x.at[1]),
        to_right("bx", spread.at[block(x_right_slot, 0)], from_x.at[0]),
    ]
    def add_y(x):
        arrive(back_y[x])
        spread[block(x, 0)] = spread[block(x, 0)] + (from_y[0, x] + from_y[1, x])

    for x in reversed(range(xslots)):
        for y in (1, 2, 0):
            if x == 0 and y == 0:
                for slot in range(1, xslots):
                    add_y(slot)
                start(back_x)
            both = dot(kron_h[block(x, y), :], back[...])
            low = dot(kron_l[block(x, y), :], back[:, 0:SZ])
            spread[block(x, y)] = both[:, 0:SZ] + (both[:, SZ : 2 * SZ] + low)
            if y > 0:
                start(back_y[x][y - 1 : y])

    add_y(0)
    arrive(back_x)
    total = spread[block(0, 0)] + (from_x[0] + from_x[1])
    restored = est[...].reshape(XY, SZ) * total / weights[...]
    out[...] = restored.reshape(SX, SY, SZ)
    for copies in [est_x, *est_y, cov_x, cov_y, cov_z, mid_z, raw_ax, raw_ay, raw_bx, raw_by, raw_az, raw_bz]:
        sent(copies)
    for copies in [*back_y, back_x, back_za, back_zb]:
        sent(copies)


def on_device(counts, estimate, raw_views, psf, offsets, coverage):
    xslots = 2 if counts[0] == 2 else 3
    group = 3 * XY
    lanes = xslots * group
    vmem = pl.BlockSpec(memory_space=pltpu.VMEM)
    smem = pl.BlockSpec(memory_space=pltpu.SMEM)
    return pl.pallas_call(
        functools.partial(kernel, counts),
        out_shape=jax.ShapeDtypeStruct(estimate.shape, F32),
        in_specs=[vmem, pl.BlockSpec(memory_space=pl.ANY), vmem, smem, smem],
        out_specs=vmem,
        scratch_shapes=[
            pltpu.VMEM((SZ, lanes), F32),
            pltpu.VMEM((2 * SZ, lanes), BF16),
            pltpu.VMEM((3, xslots, 3, 8, SZ), F32),
            pltpu.VMEM((VIEWS // 2, 32, SY, SZ), F32),
            pltpu.VMEM((VIEWS // 2, 32, SY, SZ), F32),
            pltpu.VMEM((VIEWS // 2, SX, 32, SZ), F32),
            pltpu.VMEM((VIEWS // 2, SX, 32, SZ), F32),
            pltpu.VMEM((VIEWS // 2, SZ + 16, XY), F32),
            pltpu.VMEM((VIEWS // 2, SZ + 16, XY), F32),
            pltpu.VMEM((3, 8, XY), F32),
            pltpu.VMEM((8, XY), F32),
            pltpu.VMEM((xslots + 3, 16 * VIEWS, XY), F32),
            pltpu.VMEM((lanes, VIEWS * XY), BF16),
            pltpu.VMEM((lanes, VIEWS * XY), BF16),
            pltpu.VMEM((VIEWS, 2 * SZ, ROWS), BF16),
            pltpu.VMEM((VIEWS, 2 * WIDE, SZ), BF16),
            pltpu.VMEM((VIEWS, WIDE, XY), F32),
            pltpu.VMEM((VIEWS // 2, WIDE, XY), F32),
            pltpu.VMEM((VIEWS // 2, WIDE, XY), F32),
            pltpu.VMEM((VIEWS * XY, 2 * SZ), BF16),
            pltpu.VMEM((lanes, SZ), F32),
            pltpu.VMEM((2, XY, SZ), F32),
            pltpu.VMEM((2, xslots, XY, SZ), F32),
            pltpu.VMEM((2, VIEWS // 2, 16, XY), F32),
            pltpu.VMEM((2, VIEWS // 2, 16, XY), F32),
            pltpu.VMEM((XY, SZ), F32),
            pltpu.SemaphoreType.DMA((SEMAPHORES,)),
            pltpu.SemaphoreType.DMA((SEMAPHORES,)),
            pltpu.SemaphoreType.DMA((2,)),
        ],
        compiler_params=pltpu.CompilerParams(
            collective_id=0, has_side_effects=True, vmem_limit_bytes=56 * 1024 * 1024
        ),
    )(
        estimate, raw_views, psf, offsets.T,
        coverage.transpose(1, 2, 3, 0).reshape(1, VIEWS),
    )


def solution(mesh):
    counts = (mesh.shape["bx"], mesh.shape["by"], mesh.shape["bz"])
    return jax.shard_map(
        functools.partial(on_device, counts),
        mesh=mesh,
        in_specs=(
            P("bx", "by", "bz"),
            P(None, "bx", "by", "bz"),
            P(),
            P(),
            P(None, "bx", "by", "bz"),
        ),
        out_specs=P("bx", "by", "bz"),
        check_vma=False,
    )
```
